512 devices in a mesh: gx: 4 (over y), gy: 8 (over x, core), gz: 16 (over z).
Axes of the slice: x: 4, y: 4, z: 16, core: 2. Of those that a mesh axis runs over, the one named last changes fastest.
Arguments:
- a_blocks: bfloat16 [4, 16, 32, 7, 128, 128], P('gx', 'gy', 'gz'), may hold values from -0.25 to 2
- a_cols: int32 [4, 16, 32, 7], P('gx', 'gy', 'gz'), may hold values from 0 to 2047, as said below
- p_blocks: bfloat16 [4, 16, 32, 128, 128], P('gx', 'gy', 'gz'), may hold values from -0.05 to 1.7
- agg_ids: int32 [4, 16, 32], P('gx', 'gy', 'gz'), may hold values from 0 to 1023, as said below
- coarse_cols: int32 [4, 16, 16, 11], P('gx', 'gy', 'gz'), may hold values from 0 to 1023, as said below
- coarse_rhs: float32 [4, 16, 16, 128], P('gx', 'gy', 'gz'), may hold values from -6 to 6
- coarse_start: float32 [4, 16, 16, 128], P('gx', 'gy', 'gz'), may hold values from -6 to 6
Outputs:
- coarse_solution: float32 [4, 16, 16, 128], P('gx', 'gy', 'gz')
- coarse_residual: float32 [4, 16, 16, 128], P('gx', 'gy', 'gz')
The draws below stay inside these ranges and needn't reach their ends.
Inputs may be any that keep to these rules, and one draw needn't show every extreme that they name: `a_cols`: entry [x, y, z, :] lists, in some order, the flat id of tile (x, y, z) itself and of its six face neighbours, indices taken modulo 4, 16 and 32. `agg_ids`: each column (x, y) has a phase s of 0 or 1; tile (x, y, z) belongs to aggregate (x * 16 + y) * 16 + k with k = ((z - s) mod 32) // 2, so aggregate k holds the tiles 2 k + s and 2 k + s + 1 (mod 32) of its column. `coarse_cols`: row (x, y, k) lists in slots 0, 1, 2 the aggregates k - 1, k, k + 1 (mod 16) of its own column, and in slot 3 + 2 d + j the aggregate holding the neighbour, in direction d (-x, +x, -y, +y, periodic), of its member tile j (0 the lower, 1 the upper).
All inputs are finite; a program needn't handle non-finite values.
Results may differ from the reference program's by a relative error of at most 0.00046.
Values may be sent and summed in bfloat16 or wider, within the bound.
A program may use at most 64 MiB of HBM per device.

```python
import jax
import jax.numpy as jnp
from jax import lax

B = 128
KA = 7
KC = 11
NXT = 4
NYT = 16
NZT = 32
NZH = 16


def column_phase(key):
    return jax.random.randint(jax.random.fold_in(key, 97), (NXT, NYT), 0, 2).astype(jnp.int32)


def neighbour_order(key):
    scores = jax.random.randint(jax.random.fold_in(key, 53), (NXT, NYT, NZT, KA), 0, 1 << 20) * KA + jnp.arange(KA, dtype=jnp.int32)
    return jnp.argsort(scores, axis=-1).astype(jnp.int32)


def draw_a_blocks(key, part):
    order = neighbour_order(key)
    key = jax.random.fold_in(key, 11)
    shape = (NXT, NYT, NZT, KA, B, B)
    noise = jnp.clip(jax.random.normal(key, shape, jnp.float32), -6.0, 6.0)
    own_block = (order == 0)[..., None, None]
    diagonal = jnp.where(own_block, 2.0, -0.25).astype(jnp.float32)
    spread = jnp.where(own_block, 0.01, 0.004).astype(jnp.float32)
    eye = jnp.eye(B, dtype=jnp.float32)
    return (eye * diagonal + (1.0 - eye) * spread * noise).astype(jnp.bfloat16)


def draw_p_blocks(key, part):
    key = jax.random.fold_in(key, 13)
    key_diag = jax.random.fold_in(key, 1)
    key_rest = jax.random.fold_in(key, 2)
    shape = (NXT, NYT, NZT, B, B)
    spread = 0.5 * jnp.clip(jax.random.normal(key_diag, (NXT, NYT, NZT, 1, B), jnp.float32), -1.5, 1.5)
    noise = jnp.clip(jax.random.normal(key_rest, shape, jnp.float32), -6.0, 6.0)
    eye = jnp.eye(B, dtype=jnp.float32)
    diagonal = jnp.exp2(spread)
    return (eye * diagonal + (1.0 - eye) * 0.008 * noise).astype(jnp.bfloat16)


def draw_a_cols(key, part):
    order = neighbour_order(key)
    across = jnp.arange(NXT, dtype=jnp.int32)[:, None, None, None]
    along = jnp.arange(NYT, dtype=jnp.int32)[None, :, None, None]
    depth = jnp.arange(NZT, dtype=jnp.int32)[None, None, :, None]
    shift_x = jnp.array([0, 0, 0, -1, 1, 0, 0], jnp.int32)
    shift_y = jnp.array([0, 0, 0, 0, 0, -1, 1], jnp.int32)
    shift_z = jnp.array([0, -1, 1, 0, 0, 0, 0], jnp.int32)
    ident = ((across + shift_x) % NXT * NYT + (along + shift_y) % NYT) * NZT + (depth + shift_z) % NZT
    return jnp.take_along_axis(ident, order, axis=-1).astype(jnp.int32)


def draw_agg_ids(key, part):
    phase = column_phase(key)
    across = jnp.arange(NXT, dtype=jnp.int32)[:, None, None]
    along = jnp.arange(NYT, dtype=jnp.int32)[None, :, None]
    depth = jnp.arange(NZT, dtype=jnp.int32)[None, None, :]
    layer = (depth - phase[:, :, None]) % NZT // 2
    return ((across * NYT + along) * NZH + layer).astype(jnp.int32)


def draw_coarse_cols(key, part):
    phase = column_phase(key)
    across = jnp.arange(NXT, dtype=jnp.int32)[:, None, None]
    along = jnp.arange(NYT, dtype=jnp.int32)[None, :, None]
    layer = jnp.arange(NZH, dtype=jnp.int32)[None, None, :]
    own_phase = phase[:, :, None]
    same = (across * NYT + along) * NZH
    listed = [same + (layer - 1) % NZH, same + layer + 0 * own_phase, same + (layer + 1) % NZH]
    for shift_x, shift_y in ((-1, 0), (1, 0), (0, -1), (0, 1)):
        next_x = (across + shift_x) % NXT
        next_y = (along + shift_y) % NYT
        other = phase[next_x, next_y]
        for member in (0, 1):
            depth = (2 * layer + own_phase + member) % NZT
            listed.append((next_x * NYT + next_y) * NZH + (depth - other) % NZT // 2)
    return jnp.stack(listed, axis=-1).astype(jnp.int32)


def level_of(rng, dims, cuts, least, high):
    def one(dim, parts):
        steps = jax.random.uniform(jax.random.fold_in(jax.random.fold_in(rng, 6), dim), (parts,), jnp.float32, least / len(cuts), high / len(cuts))
        return jnp.repeat(jnp.exp(steps), dims[dim] // parts).reshape((-1,) + (1,) * (len(dims) - dim - 1))

    level = one(*cuts[0])
    for cut in cuts[1:]:
        level = level * one(*cut)
    return level


def centred(rng, dims, scale, bound, split=(), kind=jnp.bfloat16):
    gain = level_of(rng, dims, split, -0.22, 0.18) if split else 1.0
    entries = jax.random.normal(rng, dims, jnp.float32) * scale * gain
    return jnp.minimum(jnp.maximum(entries, -bound), bound).astype(kind)


def setup_inputs(seed: int = 0) -> dict:
    seeds = jax.random.split(jax.random.key(seed), 8)
    a_blocks = draw_a_blocks(jax.random.fold_in(seeds[7], 71), 0)
    a_cols = draw_a_cols(jax.random.fold_in(seeds[7], 71), 0)
    p_blocks = draw_p_blocks(jax.random.fold_in(seeds[7], 71), 0)
    agg_ids = draw_agg_ids(jax.random.fold_in(seeds[7], 71), 0)
    coarse_cols = draw_coarse_cols(jax.random.fold_in(seeds[7], 71), 0)
    coarse_rhs = centred(seeds[5], (NXT, NYT, NZH, B), 1.0, 6.0, ((0, 4), (1, 8), (2, 16)), jnp.float32)
    coarse_start = centred(seeds[6], (NXT, NYT, NZH, B), 1.0, 6.0, ((0, 4), (1, 8), (2, 16)), jnp.float32)
    return {"a_blocks": a_blocks, "a_cols": a_cols, "p_blocks": p_blocks, "agg_ids": agg_ids, "coarse_cols": coarse_cols, "coarse_rhs": coarse_rhs, "coarse_start": coarse_start}


EPSILON = 1e-5


def direction_code(off_x, off_y, off_z):
    inner = jnp.where(off_y == -1, 5, jnp.where(off_y == 1, 6, 0))
    inner = jnp.where(off_x == -1, 3, jnp.where(off_x == 1, 4, inner))
    return jnp.where(off_z == -1, 1, jnp.where(off_z == 1, 2, inner)).astype(jnp.int32)


def slot_of(direction, member):
    return jnp.where(direction == 0, 1, jnp.where(direction == 1, member, jnp.where(direction == 2, 1 + member, 2 * direction - 3 + member))).astype(jnp.int32)


def wrapped(target, anchor, length):
    return (target - anchor + 1) % length - 1


def reference(a_blocks, a_cols, p_blocks, agg_ids, coarse_cols, coarse_rhs, coarse_start):
    columns = NXT * NYT
    flat_p = p_blocks.reshape(NXT * NYT * NZT, B, B)
    depth = jnp.arange(NZT, dtype=jnp.int32)

    def one_column(items):
        index, tile_a, near_ids, tile_p, tile_agg = items
        col_x = index // NYT
        col_y = index % NYT
        near = flat_p[near_ids]
        products = jnp.einsum("zenm,zeml->zenl", tile_a.astype(jnp.float32), near.astype(jnp.float32)).astype(jnp.bfloat16)
        pieces = jnp.einsum("zmn,zeml->zenl", tile_p.astype(jnp.float32), products.astype(jnp.float32))
        off_x = wrapped(near_ids // (NYT * NZT), col_x, NXT)
        off_y = wrapped((near_ids // NZT) % NYT, col_y, NYT)
        off_z = wrapped(near_ids % NZT, depth[:, None], NZT)
        direction = direction_code(off_x, off_y, off_z)
        layer = tile_agg % NZH
        phase = (0 - layer[0]) % NZH
        member = (depth - phase) % 2
        slot_index = slot_of(direction, member[:, None])
        segment = (layer[:, None] * KC + slot_index).astype(jnp.int32)
        summed = jax.ops.segment_sum(pieces.reshape(NZT * KA, B, B), segment.reshape(NZT * KA), num_segments=NZH * KC)
        return summed.reshape(NZH, KC, B, B)

    operator = lax.map(one_column, (jnp.arange(columns, dtype=jnp.int32), a_blocks.reshape(columns, NZT, KA, B, B), a_cols.reshape(columns, NZT, KA), p_blocks.reshape(columns, NZT, B, B), agg_ids.reshape(columns, NZT)))
    operator = operator.reshape(NXT * NYT * NZH, KC, B, B)
    scale = jnp.sum(jnp.abs(operator), axis=(1, 3)) + EPSILON
    column_ids = coarse_cols.reshape(NXT * NYT * NZH, KC)

    def apply(values):
        picked = values[column_ids]
        return jnp.einsum("csij,csj->ci", operator, picked, precision=lax.Precision.HIGHEST)

    right_side = coarse_rhs.reshape(-1, B)
    start = coarse_start.reshape(-1, B)
    middle = start + (right_side - apply(start)) / scale
    solution = middle + (right_side - apply(middle)) / scale
    residual = right_side - apply(solution)
    out_shape = (NXT, NYT, NZH, B)
    return solution.reshape(out_shape), residual.reshape(out_shape)
```

```python
import jax
import jax.numpy as jnp
from jax import lax
from jax.experimental import pallas as pl
from jax.experimental.pallas import tpu as pltpu
from jax.sharding import PartitionSpec as P

EPSILON = 1e-05
MESH = pl.DeviceIdType.MESH
F32 = jnp.float32
BF16 = jnp.bfloat16
N = 128
SELF, ZM, ZP, XM, XP, YM, YP = range(7)
OWN, ZED = 0, 1
LATERAL = ((-1, 0), (1, 0), (0, -1), (0, 1))
RELATIONS = (
    [(dx, dy, 0) for dx, dy in LATERAL]
    + [(0, 0, -1), (0, 0, 1)]
    + [(dx, dy, dz) for dx, dy in LATERAL for dz in (-1, 1)]
)


def opposite(r):
    return RELATIONS.index(tuple(-d for d in RELATIONS[r]))


START_TO = [0, 1, 2, 3, 4, 5, 7, 9, 11, 13]
START_FROM = [opposite(r) for r in START_TO]


def kernel(
    a_hbm, cols_ref, p_hbm, agg_ref, rhs_ref, start_ref,
    sol_ref, res_ref,
    a_v, p_v, px, py, pz, stage, partner, pieces, acc_y, acc_a,
    w_ref, m0, r0, f1, s1, r1, inv_ref, f2, s2, r2, s3, r3,
    a_sem, p_sem, bulk_send, bulk_recv, small_send, small_recv,
):
    gx, gy, gz = lax.axis_index("gx"), lax.axis_index("gy"), lax.axis_index("gz")
    nx, ny, nz = lax.axis_size("gx"), lax.axis_size("gy"), lax.axis_size("gz")
    total_y, total_z = 2 * ny, 2 * nz

    def device(r):
        dx, dy, dz = RELATIONS[r]
        return (
            lax.rem(gx + dx + nx, nx) if dx else gx,
            lax.rem(gy + dy + ny, ny) if dy else gy,
            lax.rem(gz + dz + nz, nz) if dz else gz,
        )

    devices = [device(r) for r in range(14)]
    barrier = pltpu.get_barrier_semaphore()
    for r in range(14):
        pl.semaphore_signal(barrier, inc=1, device_id=devices[r], device_id_type=MESH)

    p_copy = pltpu.make_async_copy(p_hbm.at[0], p_v, p_sem)
    p_copy.start()
    a_copy = pltpu.make_async_copy(a_hbm.at[0], a_v, a_sem)
    a_copy.start()

    phase = [
        (agg_ref[0, c, 0] != (gx * total_y + 2 * gy + c) * nz + gz).astype(jnp.int32)
        for c in (0, 1)
    ]

    def place(c, j, d):
        dx = {XM: -1, XP: 1}.get(d, 0)
        dy = {YM: -1, YP: 1}.get(d, 0)
        dz = {ZM: -1, ZP: 1}.get(d, 0)
        x = lax.rem(gx + dx + nx, nx)
        y = lax.rem(2 * gy + c + dy + total_y, total_y)
        z = lax.rem(2 * gz + j + dz + total_z, total_z)
        want = (x * total_y + y) * total_z + z
        found = jnp.int32(0)
        for e in range(1, 7):
            found = jnp.where(cols_ref[0, c, j, e] == want, e, found)
        return found

    row8 = lax.broadcasted_iota(jnp.int32, (8, N), 0)
    even8 = lax.rem(row8, 2) == 0
    even4 = even8[0:4]
    ph8 = jnp.where(lax.rem(row8, 4) < 2, phase[0], phase[1]).astype(F32)
    ph4 = ph8[0:4]
    straddle8 = ph8 > 0.5
    straddle4 = ph4 > 0.5
    start = start_ref[0, :, 0, :]
    for c in (0, 1):
        m0[0, 2 * c : 2 * c + 1, :] = start[c : c + 1]
        m0[0, 2 * c + 1 : 2 * c + 2, :] = start[c : c + 1]
    m0[0, 4:8, :] = jnp.zeros((4, N), F32)
    m0[1] = ph8

    pl.semaphore_wait(barrier, 14)

    small = [
        pltpu.make_async_remote_copy(
            m0, r0.at[START_FROM.index(opposite(r))], small_send.at[0], small_recv.at[0],
            device_id=devices[r], device_id_type=MESH,
        )
        for r in START_TO
    ]
    for copy in small:
        copy.start()

    def bulk(k, source, target, r):
        return pltpu.make_async_remote_copy(
            source, target, bulk_send.at[k], bulk_recv.at[k],
            device_id=devices[r], device_id_type=MESH,
        )

    sends = [
        bulk(0, p_hbm.at[0, :, 1], pz.at[0], 5),
        bulk(1, p_hbm.at[0, :, 0], pz.at[1], 4),
        bulk(2, p_hbm.at[0], px.at[0], 1),
        bulk(3, p_hbm.at[0], px.at[1], 0),
        bulk(4, p_hbm.at[0, 1], py.at[0], 3),
        bulk(5, p_hbm.at[0, 0], py.at[1], 2),
        bulk(6, stage.at[0], partner.at[0], 4),
        bulk(7, stage.at[1], partner.at[1], 5),
    ]
    for copy in sends[:6]:
        copy.start()

    where = [[[place(c, j, d) for d in range(7)] for j in (0, 1)] for c in (0, 1)]

    a_copy.wait()
    stage[0, 0] = a_v[0, 0, where[0][0][SELF]]
    stage[0, 1] = a_v[0, 0, where[0][0][ZM]]
    stage[1, 0] = a_v[1, 1, where[1][1][SELF]]
    stage[1, 1] = a_v[1, 1, where[1][1][ZP]]
    sends[6].start()
    sends[7].start()

    pltpu.make_async_copy(r0, r0, small_recv.at[0]).wait()
    below, above = r0[START_FROM.index(4), 0, 0:4], r0[START_FROM.index(5), 0, 0:4]
    mine = m0[0, 0:4]
    w_ref[OWN, 0:4] = jnp.where(straddle4 & even4, below, mine)
    w_ref[ZED, 0:4] = jnp.where(even4, below, jnp.where(straddle4, mine, above))
    for l in range(4):
        side = START_FROM.index(l)
        far = START_FROM.index(6 + 2 * l)
        moved = (r0[side, 1, 0:4] > 0.5) & even4
        w_ref[2 + l, 0:4] = jnp.where(moved, r0[far, 0, 0:4], r0[side, 0, 0:4])

    def vector(c, j, d):
        t = 2 * c + j
        if d == SELF:
            block, row = OWN, t
        elif d in (ZM, ZP):
            inner = (d == ZP) == (j == 0)
            block, row = (OWN, 2 * c + 1 - j) if inner else (ZED, t)
        elif d in (XM, XP):
            block, row = 2 + (d - XM), t
        else:
            inner = (d == YP) == (c == 0)
            block, row = (OWN, 2 * (1 - c) + j) if inner else (4 + (d - YM), 2 * (1 - c) + j)
        return w_ref[block, row : row + 1, :]

    def near(c, j, d):
        if d == SELF:
            return p_v[c, j]
        if d in (ZM, ZP):
            inner = (d == ZP) == (j == 0)
            return p_v[c, 1 - j] if inner else pz[0 if d == ZM else 1, c]
        if d in (XM, XP):
            return px[d - XM, c, j]
        inner = (d == YP) == (c == 0)
        return p_v[1 - c, j] if inner else py[d - YM, j]

    def dot(a, b):
        return jnp.dot(a, b, preferred_element_type=F32)

    eye = lax.broadcasted_iota(jnp.int32, (N, N), 0) == lax.broadcasted_iota(
        jnp.int32, (N, N), 1
    )

    def row_sums(block):
        total = jnp.sum(block, axis=1, keepdims=True)
        return jnp.sum(jnp.where(eye, total, 0.0), axis=0, keepdims=True)

    p_copy.wait()
    flipped = [[p_v[c, j].T for j in (0, 1)] for c in (0, 1)]

    def piece(c, j, d):
        block = a_v[c, j, where[c][j][d]]
        result = dot(flipped[c][j], dot(block, near(c, j, d)).astype(BF16))
        t = 2 * c + j
        pieces[t, d] = result
        return result

    INNER_Z = (ZP, ZM)
    OUTER_Z = (ZM, ZP)
    for c in (0, 1):
        for j in (0, 1):
            t = 2 * c + j
            inner_y = YP if c == 0 else YM
            y = piece(c, j, SELF) * vector(c, j, SELF)
            y += piece(c, j, INNER_Z[j]) * vector(c, j, INNER_Z[j])
            lateral = piece(c, j, inner_y)
            acc_y[t] = y + lateral * vector(c, j, inner_y)
            acc_a[t] = jnp.abs(lateral)

    sends[0].wait_recv()
    sends[1].wait_recv()
    for c in (0, 1):
        for j in (0, 1):
            t = 2 * c + j
            acc_y[t] += piece(c, j, OUTER_Z[j]) * vector(c, j, OUTER_Z[j])

    sends[6].wait_recv()
    sends[7].wait_recv()
    for c in (0, 1):
        j = 1 - c
        other = pz[1 - c, c]
        mid_self = dot(partner[c, 0], other).astype(BF16)
        mid_outer = dot(partner[c, 1], p_v[c, j]).astype(BF16)
        turned = other.T
        far = dot(turned, mid_self) + dot(turned, mid_outer)
        t = 2 * c + j
        split = pieces[t, SELF] + pieces[t, OUTER_Z[j]] + far
        whole = (pieces[2 * c, SELF] + pieces[2 * c, ZP]) + (
            pieces[2 * c + 1, SELF] + pieces[2 * c + 1, ZM]
        )
        acc_a[t] += jnp.abs(jnp.where(phase[c] == 1, split, whole))
        for i in (0, 1):
            t = 2 * c + i
            acc_a[t] += jnp.abs(
                jnp.where(phase[c] == 1, pieces[t, INNER_Z[i]], pieces[t, OUTER_Z[i]])
            )

    sends[4].wait_recv()
    sends[5].wait_recv()
    for c in (0, 1):
        d = YM if c == 0 else YP
        for j in (0, 1):
            t = 2 * c + j
            lateral = piece(c, j, d)
            acc_y[t] += lateral * vector(c, j, d)
            acc_a[t] += jnp.abs(lateral)

    sends[2].wait_recv()
    sends[3].wait_recv()
    sums, scales = [], []
    for c in (0, 1):
        for j in (0, 1):
            t = 2 * c + j
            low, high = piece(c, j, XM), piece(c, j, XP)
            sums.append(row_sums(acc_y[t] + low * vector(c, j, XM) + high * vector(c, j, XP)))
            scales.append(row_sums(acc_a[t] + jnp.abs(low) + jnp.abs(high)))

    rhs = rhs_ref[0, :, 0, :]

    def parts(c, lower, upper, extra):
        whole = extra + lower + upper
        split = phase[c] == 1
        return jnp.where(split, lower, whole), jnp.where(split, extra + upper, whole)

    def defects(c, sums):
        return parts(c, -sums[2 * c], -sums[2 * c + 1], rhs[c : c + 1])

    def put(full, swapped, base, pair):
        full[base : base + 1, :] = pair[0]
        full[base + 1 : base + 2, :] = pair[1]
        swapped[base : base + 1, :] = pair[1]
        swapped[base + 1 : base + 2, :] = pair[0]

    def exchange(k, full, swapped, target):
        copies = [
            pltpu.make_async_remote_copy(
                full if r < 4 else swapped, target.at[opposite(r)],
                small_send.at[k], small_recv.at[k],
                device_id=devices[r], device_id_type=MESH,
            )
            for r in range(14)
        ]
        for copy in copies:
            copy.start()
        pltpu.make_async_copy(target, target, small_recv.at[k]).wait()

    def combined(full, target, even, straddle):
        crossing = jnp.where(even, target[4], target[5])
        own = full[...]
        own = own + jnp.where(straddle, crossing, 0.0)
        out = [own, jnp.where(straddle, own, crossing)]
        for l in range(4):
            far = jnp.where(even, target[6 + 2 * l], target[7 + 2 * l])
            moved = r0[START_FROM.index(l), 1, 0 : even.shape[0]] > 0.5
            out.append(target[l] + jnp.where(moved, far, 0.0))
        return out

    for c in (0, 1):
        put(f1, s1, 2 * c, defects(c, sums))
        put(f1, s1, 4 + 2 * c, parts(c, scales[2 * c], scales[2 * c + 1], EPSILON))
    exchange(1, f1, s1, r1)
    for k, total in enumerate(combined(f1, r1, even8, straddle8)):
        inverse = 1.0 / total[4:8]
        inv_ref[k, 0:4] = inverse
        w_ref[k, 0:4] = w_ref[k, 0:4] + total[0:4] * inverse

    def apply_coarse():
        out = []
        for c in (0, 1):
            for j in (0, 1):
                t = 2 * c + j
                acc = pieces[t, 0] * vector(c, j, 0)
                for d in range(1, 7):
                    acc += pieces[t, d] * vector(c, j, d)
                out.append(row_sums(acc))
        return out

    sums = apply_coarse()
    for c in (0, 1):
        put(f2, s2, 2 * c, defects(c, sums))
    exchange(2, f2, s2, r2)
    for k, total in enumerate(combined(f2, r2, even4, straddle4)):
        w_ref[k, 0:4] = w_ref[k, 0:4] + total * inv_ref[k, 0:4]

    sums = apply_coarse()
    last = [defects(c, sums) for c in (0, 1)]
    for c in (0, 1):
        s3[c : c + 1, :] = last[c][0]
    down = pltpu.make_async_remote_copy(
        s3, r3, small_send.at[3], small_recv.at[3], device_id=devices[4], device_id_type=MESH
    )
    down.start()
    for c in (0, 1):
        sol_ref[0, c, :, :] = w_ref[OWN, 2 * c + 1 : 2 * c + 2, :]
    down.wait_recv()
    for c in (0, 1):
        res_ref[0, c, :, :] = last[c][1] + jnp.where(phase[c] == 1, r3[c : c + 1, :], 0.0)

    down.wait_send()
    pltpu.make_async_copy(r0, r0, small_send.at[0]).wait()
    pltpu.make_async_copy(r1, r1, small_send.at[1]).wait()
    pltpu.make_async_copy(r2, r2, small_send.at[2]).wait()
    for copy in sends:
        copy.wait_send()


def body(a_blocks, a_cols, p_blocks, agg_ids, coarse_cols, coarse_rhs, coarse_start):
    del coarse_cols
    vmem = pl.BlockSpec(memory_space=pltpu.VMEM)
    smem = pl.BlockSpec(memory_space=pltpu.SMEM)
    hbm = pl.BlockSpec(memory_space=pl.ANY)
    shape = jax.ShapeDtypeStruct(coarse_rhs.shape, F32)
    return pl.pallas_call(
        kernel,
        out_shape=(shape, shape),
        in_specs=[hbm, smem, hbm, smem, vmem, vmem],
        out_specs=(vmem, vmem),
        scratch_shapes=[
            pltpu.VMEM((2, 2, 7, N, N), BF16),
            pltpu.VMEM((2, 2, N, N), BF16),
            pltpu.VMEM((2, 2, 2, N, N), BF16),
            pltpu.VMEM((2, 2, N, N), BF16),
            pltpu.VMEM((2, 2, N, N), BF16),
            pltpu.VMEM((2, 2, N, N), BF16),
            pltpu.VMEM((2, 2, N, N), BF16),
            pltpu.VMEM((4, 7, N, N), F32),
            pltpu.VMEM((4, N, N), F32),
            pltpu.VMEM((4, N, N), F32),
            pltpu.VMEM((6, 8, N), F32),
            pltpu.VMEM((2, 8, N), F32),
            pltpu.VMEM((10, 2, 8, N), F32),
            pltpu.VMEM((8, N), F32),
            pltpu.VMEM((8, N), F32),
            pltpu.VMEM((14, 8, N), F32),
            pltpu.VMEM((6, 8, N), F32),
            pltpu.VMEM((4, N), F32),
            pltpu.VMEM((4, N), F32),
            pltpu.VMEM((14, 4, N), F32),
            pltpu.VMEM((2, N), F32),
            pltpu.VMEM((2, N), F32),
            pltpu.SemaphoreType.DMA,
            pltpu.SemaphoreType.DMA,
            pltpu.SemaphoreType.DMA((8,)),
            pltpu.SemaphoreType.DMA((8,)),
            pltpu.SemaphoreType.DMA((4,)),
            pltpu.SemaphoreType.DMA((4,)),
        ],
        compiler_params=pltpu.CompilerParams(
            collective_id=0, has_side_effects=True, vmem_limit_bytes=32 * 2**20
        ),
        name="coarse_setup",
    )(a_blocks, a_cols, p_blocks, agg_ids, coarse_rhs, coarse_start)


def solution(mesh):
    return jax.shard_map(
        body,
        mesh=mesh,
        in_specs=(
            P("gx", "gy", "gz", None, None, None),
            P("gx", "gy", "gz", None),
            P("gx", "gy", "gz", None, None),
            P("gx", "gy", "gz"),
            P("gx", "gy", "gz", None),
            P("gx", "gy", "gz", None),
            P("gx", "gy", "gz", None),
        ),
        out_specs=(P("gx", "gy", "gz", None), P("gx", "gy", "gz", None)),
        check_vma=False,
    )
```

```python
import jax
import jax.numpy as jnp
from jax import lax
from jax.experimental import pallas as pl
from jax.experimental.pallas import tpu as pltpu
from jax.sharding import PartitionSpec as P

EPSILON = 1e-05
MESH = pl.DeviceIdType.MESH
F32 = jnp.float32
BF16 = jnp.bfloat16
N = 128
SELF, ZM, ZP, XM, XP, YM, YP = range(7)
OWN, ZED = 0, 1
LATERAL = ((-1, 0), (1, 0), (0, -1), (0, 1))
RELATIONS = (
    [(dx, dy, 0) for dx, dy in LATERAL]
    + [(0, 0, -1), (0, 0, 1)]
    + [(dx, dy, dz) for dx, dy in LATERAL for dz in (-1, 1)]
)


def opposite(r):
    return RELATIONS.index(tuple(-d for d in RELATIONS[r]))


START_TO = [0, 1, 2, 3, 4, 5, 7, 9, 11, 13]
START_FROM = [opposite(r) for r in START_TO]


def kernel(
    a_hbm, cols_hbm, p_hbm, agg_hbm, rhs_hbm, start_hbm,
    out_ref,
    cols_ref, agg_ref, rhs_ref, start_ref,
    a_v, p_v, px, py, pz, stage, partner, pieces, acc_y, acc_a,
    w_ref, m0, r0, f1, s1, r1, inv_ref, f2, s2, r2, s3, r3,
    a_sem, p_sem, in_sem, bulk_send, bulk_recv, small_send, small_recv,
):
    gx, gy, gz = lax.axis_index("gx"), lax.axis_index("gy"), lax.axis_index("gz")
    nx, ny, nz = lax.axis_size("gx"), lax.axis_size("gy"), lax.axis_size("gz")
    total_y, total_z = 2 * ny, 2 * nz

    def device(r):
        dx, dy, dz = RELATIONS[r]
        return (
            lax.rem(gx + dx + nx, nx) if dx else gx,
            lax.rem(gy + dy + ny, ny) if dy else gy,
            lax.rem(gz + dz + nz, nz) if dz else gz,
        )

    devices = [device(r) for r in range(14)]
    barrier = pltpu.get_barrier_semaphore()
    for r in range(14):
        pl.semaphore_signal(barrier, inc=1, device_id=devices[r], device_id_type=MESH)

    inputs = [
        pltpu.make_async_copy(source, target, in_sem.at[k])
        for k, (source, target) in enumerate(
            ((agg_hbm, agg_ref), (start_hbm, start_ref), (cols_hbm, cols_ref), (rhs_hbm, rhs_ref))
        )
    ]
    for copy in inputs:
        copy.start()
    p_copy = pltpu.make_async_copy(p_hbm.at[0], p_v, p_sem)
    p_copy.start()
    a_copy = pltpu.make_async_copy(a_hbm.at[0], a_v, a_sem)
    a_copy.start()

    for copy in inputs:
        copy.wait()

    phase = [
        (agg_ref[0, c, 0] != (gx * total_y + 2 * gy + c) * nz + gz).astype(jnp.int32)
        for c in (0, 1)
    ]

    def place(c, j, d):
        dx = {XM: -1, XP: 1}.get(d, 0)
        dy = {YM: -1, YP: 1}.get(d, 0)
        dz = {ZM: -1, ZP: 1}.get(d, 0)
        x = lax.rem(gx + dx + nx, nx)
        y = lax.rem(2 * gy + c + dy + total_y, total_y)
        z = lax.rem(2 * gz + j + dz + total_z, total_z)
        want = (x * total_y + y) * total_z + z
        found = jnp.int32(0)
        for e in range(1, 7):
            found = jnp.where(cols_ref[0, c, j, e] == want, e, found)
        return found

    row8 = lax.broadcasted_iota(jnp.int32, (8, N), 0)
    even8 = lax.rem(row8, 2) == 0
    even4 = even8[0:4]
    ph8 = jnp.where(lax.rem(row8, 4) < 2, phase[0], phase[1]).astype(F32)
    ph4 = ph8[0:4]
    straddle8 = ph8 > 0.5
    straddle4 = ph4 > 0.5
    start = start_ref[0, :, 0, :]
    for c in (0, 1):
        m0[0, 2 * c : 2 * c + 1, :] = start[c : c + 1]
        m0[0, 2 * c + 1 : 2 * c + 2, :] = start[c : c + 1]
    m0[0, 4:8, :] = jnp.zeros((4, N), F32)
    m0[1] = ph8

    pl.semaphore_wait(barrier, 14)

    small = [
        pltpu.make_async_remote_copy(
            m0, r0.at[START_FROM.index(opposite(r))], small_send.at[0], small_recv.at[0],
            device_id=devices[r], device_id_type=MESH,
        )
        for r in START_TO
    ]
    for copy in small:
        copy.start()

    def bulk(k, source, target, r):
        return pltpu.make_async_remote_copy(
            source, target, bulk_send.at[k], bulk_recv.at[k],
            device_id=devices[r], device_id_type=MESH,
        )

    sends = [
        bulk(0, p_hbm.at[0, :, 1], pz.at[0], 5),
        bulk(1, p_hbm.at[0, :, 0], pz.at[1], 4),
        bulk(2, p_hbm.at[0], px.at[0], 1),
        bulk(3, p_hbm.at[0], px.at[1], 0),
        bulk(4, p_hbm.at[0, 1], py.at[0], 3),
        bulk(5, p_hbm.at[0, 0], py.at[1], 2),
        bulk(6, stage.at[0], partner.at[0], 4),
        bulk(7, stage.at[1], partner.at[1], 5),
    ]
    for copy in sends[:6]:
        copy.start()

    where = [[[place(c, j, d) for d in range(7)] for j in (0, 1)] for c in (0, 1)]

    a_copy.wait()
    stage[0, 0] = a_v[0, 0, where[0][0][SELF]]
    stage[0, 1] = a_v[0, 0, where[0][0][ZM]]
    stage[1, 0] = a_v[1, 1, where[1][1][SELF]]
    stage[1, 1] = a_v[1, 1, where[1][1][ZP]]
    sends[6].start()
    sends[7].start()

    pltpu.make_async_copy(r0, r0, small_recv.at[0]).wait()
    below, above = r0[START_FROM.index(4), 0, 0:4], r0[START_FROM.index(5), 0, 0:4]
    mine = m0[0, 0:4]
    w_ref[OWN, 0:4] = jnp.where(straddle4 & even4, below, mine)
    w_ref[ZED, 0:4] = jnp.where(even4, below, jnp.where(straddle4, mine, above))
    for l in range(4):
        side = START_FROM.index(l)
        far = START_FROM.index(6 + 2 * l)
        moved = (r0[side, 1, 0:4] > 0.5) & even4
        w_ref[2 + l, 0:4] = jnp.where(moved, r0[far, 0, 0:4], r0[side, 0, 0:4])

    def vector(c, j, d):
        t = 2 * c + j
        if d == SELF:
            block, row = OWN, t
        elif d in (ZM, ZP):
            inner = (d == ZP) == (j == 0)
            block, row = (OWN, 2 * c + 1 - j) if inner else (ZED, t)
        elif d in (XM, XP):
            block, row = 2 + (d - XM), t
        else:
            inner = (d == YP) == (c == 0)
            block, row = (OWN, 2 * (1 - c) + j) if inner else (4 + (d - YM), 2 * (1 - c) + j)
        return w_ref[block, row : row + 1, :]

    def near(c, j, d):
        if d == SELF:
            return p_v[c, j]
        if d in (ZM, ZP):
            inner = (d == ZP) == (j == 0)
            return p_v[c, 1 - j] if inner else pz[0 if d == ZM else 1, c]
        if d in (XM, XP):
            return px[d - XM, c, j]
        inner = (d == YP) == (c == 0)
        return p_v[1 - c, j] if inner else py[d - YM, j]

    def dot(a, b):
        return jnp.dot(a, b, preferred_element_type=F32)

    eye = lax.broadcasted_iota(jnp.int32, (N, N), 0) == lax.broadcasted_iota(
        jnp.int32, (N, N), 1
    )

    def row_sums(block):
        total = jnp.sum(block, axis=1, keepdims=True)
        return jnp.sum(jnp.where(eye, total, 0.0), axis=0, keepdims=True)

    p_copy.wait()
    flipped = [[p_v[c, j].T for j in (0, 1)] for c in (0, 1)]

    def piece(c, j, d):
        block = a_v[c, j, where[c][j][d]]
        result = dot(flipped[c][j], dot(block, near(c, j, d)).astype(BF16))
        t = 2 * c + j
        pieces[t, d] = result
        return result

    INNER_Z = (ZP, ZM)
    OUTER_Z = (ZM, ZP)
    for c in (0, 1):
        for j in (0, 1):
            t = 2 * c + j
            inner_y = YP if c == 0 else YM
            y = piece(c, j, SELF) * vector(c, j, SELF)
            y += piece(c, j, INNER_Z[j]) * vector(c, j, INNER_Z[j])
            lateral = piece(c, j, inner_y)
            acc_y[t] = y + lateral * vector(c, j, inner_y)
            acc_a[t] = jnp.abs(lateral)

    sends[0].wait_recv()
    sends[1].wait_recv()
    for c in (0, 1):
        for j in (0, 1):
            t = 2 * c + j
            acc_y[t] += piece(c, j, OUTER_Z[j]) * vector(c, j, OUTER_Z[j])

    sends[6].wait_recv()
    sends[7].wait_recv()
    for c in (0, 1):
        j = 1 - c
        other = pz[1 - c, c]
        mid_self = dot(partner[c, 0], other).astype(BF16)
        mid_outer = dot(partner[c, 1], p_v[c, j]).astype(BF16)
        turned = other.T
        far = dot(turned, mid_self) + dot(turned, mid_outer)
        t = 2 * c + j
        split = pieces[t, SELF] + pieces[t, OUTER_Z[j]] + far
        whole = (pieces[2 * c, SELF] + pieces[2 * c, ZP]) + (
            pieces[2 * c + 1, SELF] + pieces[2 * c + 1, ZM]
        )
        acc_a[t] += jnp.abs(jnp.where(phase[c] == 1, split, whole))
        for i in (0, 1):
            t = 2 * c + i
            acc_a[t] += jnp.abs(
                jnp.where(phase[c] == 1, pieces[t, INNER_Z[i]], pieces[t, OUTER_Z[i]])
            )

    sends[4].wait_recv()
    sends[5].wait_recv()
    for c in (0, 1):
        d = YM if c == 0 else YP
        for j in (0, 1):
            t = 2 * c + j
            lateral = piece(c, j, d)
            acc_y[t] += lateral * vector(c, j, d)
            acc_a[t] += jnp.abs(lateral)

    sends[2].wait_recv()
    sends[3].wait_recv()
    sums, scales = [], []
    for c in (0, 1):
        for j in (0, 1):
            t = 2 * c + j
            low, high = piece(c, j, XM), piece(c, j, XP)
            sums.append(row_sums(acc_y[t] + low * vector(c, j, XM) + high * vector(c, j, XP)))
            scales.append(row_sums(acc_a[t] + jnp.abs(low) + jnp.abs(high)))

    rhs = rhs_ref[0, :, 0, :]

    def parts(c, lower, upper, extra):
        whole = extra + lower + upper
        split = phase[c] == 1
        return jnp.where(split, lower, whole), jnp.where(split, extra + upper, whole)

    def defects(c, sums):
        return parts(c, -sums[2 * c], -sums[2 * c + 1], rhs[c : c + 1])

    def put(full, swapped, base, pair):
        full[base : base + 1, :] = pair[0]
        full[base + 1 : base + 2, :] = pair[1]
        swapped[base : base + 1, :] = pair[1]
        swapped[base + 1 : base + 2, :] = pair[0]

    def exchange(k, full, swapped, target):
        copies = [
            pltpu.make_async_remote_copy(
                full if r < 4 else swapped, target.at[opposite(r)],
                small_send.at[k], small_recv.at[k],
                device_id=devices[r], device_id_type=MESH,
            )
            for r in range(14)
        ]
        for copy in copies:
            copy.start()
        pltpu.make_async_copy(target, target, small_recv.at[k]).wait()

    def combined(full, target, even, straddle):
        crossing = jnp.where(even, target[4], target[5])
        own = full[...]
        own = own + jnp.where(straddle, crossing, 0.0)
        out = [own, jnp.where(straddle, own, crossing)]
        for l in range(4):
            far = jnp.where(even, target[6 + 2 * l], target[7 + 2 * l])
            moved = r0[START_FROM.index(l), 1, 0 : even.shape[0]] > 0.5
            out.append(target[l] + jnp.where(moved, far, 0.0))
        return out

    for c in (0, 1):
        put(f1, s1, 2 * c, defects(c, sums))
        put(f1, s1, 4 + 2 * c, parts(c, scales[2 * c], scales[2 * c + 1], EPSILON))
    exchange(1, f1, s1, r1)
    for k, total in enumerate(combined(f1, r1, even8, straddle8)):
        inverse = 1.0 / total[4:8]
        inv_ref[k, 0:4] = inverse
        w_ref[k, 0:4] = w_ref[k, 0:4] + total[0:4] * inverse

    def apply_coarse():
        out = []
        for c in (0, 1):
            for j in (0, 1):
                t = 2 * c + j
                acc = pieces[t, 0] * vector(c, j, 0)
                for d in range(1, 7):
                    acc += pieces[t, d] * vector(c, j, d)
                out.append(row_sums(acc))
        return out

    sums = apply_coarse()
    for c in (0, 1):
        put(f2, s2, 2 * c, defects(c, sums))
    exchange(2, f2, s2, r2)
    for k, total in enumerate(combined(f2, r2, even4, straddle4)):
        w_ref[k, 0:4] = w_ref[k, 0:4] + total * inv_ref[k, 0:4]

    sums = apply_coarse()
    last = [defects(c, sums) for c in (0, 1)]
    for c in (0, 1):
        s3[c : c + 1, :] = last[c][0]
    down = pltpu.make_async_remote_copy(
        s3, r3, small_send.at[3], small_recv.at[3], device_id=devices[4], device_id_type=MESH
    )
    down.start()
    for c in (0, 1):
        out_ref[0, c, 0:1, :] = w_ref[OWN, 2 * c + 1 : 2 * c + 2, :]
    down.wait_recv()
    for c in (0, 1):
        out_ref[0, c, 1:2, :] = last[c][1] + jnp.where(phase[c] == 1, r3[c : c + 1, :], 0.0)

    down.wait_send()
    pltpu.make_async_copy(r0, r0, small_send.at[0]).wait()
    pltpu.make_async_copy(r1, r1, small_send.at[1]).wait()
    pltpu.make_async_copy(r2, r2, small_send.at[2]).wait()
    for copy in sends:
        copy.wait_send()


def body(a_blocks, a_cols, p_blocks, agg_ids, coarse_cols, coarse_rhs, coarse_start):
    del coarse_cols
    vmem = pl.BlockSpec(memory_space=pltpu.VMEM)
    hbm = pl.BlockSpec(memory_space=pltpu.HBM)
    one, rows, layers, width = coarse_rhs.shape
    out = pl.pallas_call(
        kernel,
        out_shape=jax.ShapeDtypeStruct((one, rows, 2 * layers, width), F32),
        in_specs=[hbm] * 6,
        out_specs=vmem,
        scratch_shapes=[
            pltpu.SMEM(a_cols.shape, jnp.int32),
            pltpu.SMEM(agg_ids.shape, jnp.int32),
            pltpu.VMEM(coarse_rhs.shape, F32),
            pltpu.VMEM(coarse_start.shape, F32),
            pltpu.VMEM((2, 2, 7, N, N), BF16),
            pltpu.VMEM((2, 2, N, N), BF16),
            pltpu.VMEM((2, 2, 2, N, N), BF16),
            pltpu.VMEM((2, 2, N, N), BF16),
            pltpu.VMEM((2, 2, N, N), BF16),
            pltpu.VMEM((2, 2, N, N), BF16),
            pltpu.VMEM((2, 2, N, N), BF16),
            pltpu.VMEM((4, 7, N, N), F32),
            pltpu.VMEM((4, N, N), F32),
            pltpu.VMEM((4, N, N), F32),
            pltpu.VMEM((6, 8, N), F32),
            pltpu.VMEM((2, 8, N), F32),
            pltpu.VMEM((10, 2, 8, N), F32),
            pltpu.VMEM((8, N), F32),
            pltpu.VMEM((8, N), F32),
            pltpu.VMEM((14, 8, N), F32),
            pltpu.VMEM((6, 8, N), F32),
            pltpu.VMEM((4, N), F32),
            pltpu.VMEM((4, N), F32),
            pltpu.VMEM((14, 4, N), F32),
            pltpu.VMEM((2, N), F32),
            pltpu.VMEM((2, N), F32),
            pltpu.SemaphoreType.DMA,
            pltpu.SemaphoreType.DMA,
            pltpu.SemaphoreType.DMA((4,)),
            pltpu.SemaphoreType.DMA((8,)),
            pltpu.SemaphoreType.DMA((8,)),
            pltpu.SemaphoreType.DMA((4,)),
            pltpu.SemaphoreType.DMA((4,)),
        ],
        compiler_params=pltpu.CompilerParams(
            collective_id=0, has_side_effects=True, vmem_limit_bytes=63 * 2**20
        ),
        name="coarse_setup",
    )(a_blocks, a_cols, p_blocks, agg_ids, coarse_rhs, coarse_start)
    return out[:, :, 0:1], out[:, :, 1:2]


def solution(mesh):
    return jax.shard_map(
        body,
        mesh=mesh,
        in_specs=(
            P("gx", "gy", "gz", None, None, None),
            P("gx", "gy", "gz", None),
            P("gx", "gy", "gz", None, None),
            P("gx", "gy", "gz"),
            P("gx", "gy", "gz", None),
            P("gx", "gy", "gz", None),
            P("gx", "gy", "gz", None),
        ),
        out_specs=(P("gx", "gy", "gz", None), P("gx", "gy", "gz", None)),
        check_vma=False,
    )
```

```python
import jax
import jax.numpy as jnp
from jax import lax
from jax.experimental import pallas as pl
from jax.experimental.pallas import tpu as pltpu
from jax.sharding import PartitionSpec as P

EPSILON = 1e-05
MESH = pl.DeviceIdType.MESH
F32 = jnp.float32
BF16 = jnp.bfloat16
N = 128
SELF, ZM, ZP, XM, XP, YM, YP = range(7)
OWN, ZED = 0, 1
LATERAL = ((-1, 0), (1, 0), (0, -1), (0, 1))
RELATIONS = (
    [(dx, dy, 0) for dx, dy in LATERAL]
    + [(0, 0, -1), (0, 0, 1)]
    + [(dx, dy, dz) for dx, dy in LATERAL for dz in (-1, 1)]
)


def opposite(r):
    return RELATIONS.index(tuple(-d for d in RELATIONS[r]))


FACES = range(6)
UPWARD = (7, 9, 11, 13)
ORDER = list(range(6, 14)) + [4, 5, 0, 1, 2, 3]


def kernel(
    a_hbm, cols_hbm, p_hbm, agg_hbm, rhs_hbm, start_hbm,
    out_ref,
    cols_ref, agg_ref, rhs_ref, start_ref,
    a_v, p_v, px, py, pz, stage, partner, pieces, acc_a,
    w_ref, m0, r0, d0, f1, s1, r1, inv_ref, f2, s2, r2, s3, r3,
    a_sem, p_sem, in_sem, bulk_send, bulk_recv, small_send, small_recv, far_send, far_recv,
):
    gx, gy, gz = lax.axis_index("gx"), lax.axis_index("gy"), lax.axis_index("gz")
    nx, ny, nz = lax.axis_size("gx"), lax.axis_size("gy"), lax.axis_size("gz")
    total_y, total_z = 2 * ny, 2 * nz

    def device(r):
        dx, dy, dz = RELATIONS[r]
        return (
            lax.rem(gx + dx + nx, nx) if dx else gx,
            lax.rem(gy + dy + ny, ny) if dy else gy,
            lax.rem(gz + dz + nz, nz) if dz else gz,
        )

    devices = [device(r) for r in range(14)]
    barrier = pltpu.get_barrier_semaphore()
    for r in (6, 8, 10, 12, *FACES):
        pl.semaphore_signal(barrier, inc=1, device_id=devices[r], device_id_type=MESH)

    inputs = [
        pltpu.make_async_copy(source, target, in_sem.at[k])
        for k, (source, target) in enumerate(
            ((agg_hbm, agg_ref), (start_hbm, start_ref), (cols_hbm, cols_ref), (rhs_hbm, rhs_ref))
        )
    ]
    for copy in inputs:
        copy.start()
    p_copy = pltpu.make_async_copy(p_hbm.at[0], p_v, p_sem)
    p_copy.start()
    a_copy = pltpu.make_async_copy(a_hbm.at[0], a_v, a_sem)
    a_copy.start()

    for copy in inputs:
        copy.wait()

    phase = [
        (agg_ref[0, c, 0] != (gx * total_y + 2 * gy + c) * nz + gz).astype(jnp.int32)
        for c in (0, 1)
    ]

    def place(c, j, d):
        dx = {XM: -1, XP: 1}.get(d, 0)
        dy = {YM: -1, YP: 1}.get(d, 0)
        dz = {ZM: -1, ZP: 1}.get(d, 0)
        x = lax.rem(gx + dx + nx, nx)
        y = lax.rem(2 * gy + c + dy + total_y, total_y)
        z = lax.rem(2 * gz + j + dz + total_z, total_z)
        want = (x * total_y + y) * total_z + z
        found = jnp.int32(0)
        for e in range(1, 7):
            found = jnp.where(cols_ref[0, c, j, e] == want, e, found)
        return found

    row8 = lax.broadcasted_iota(jnp.int32, (8, N), 0)
    even8 = lax.rem(row8, 2) == 0
    even4 = even8[0:4]
    ph8 = jnp.where(lax.rem(row8, 4) < 2, phase[0], phase[1]).astype(F32)
    ph4 = ph8[0:4]
    straddle8 = ph8 > 0.5
    straddle4 = ph4 > 0.5
    start = start_ref[0, :, 0, :]
    for c in (0, 1):
        m0[0, 2 * c : 2 * c + 1, :] = start[c : c + 1]
        m0[0, 2 * c + 1 : 2 * c + 2, :] = start[c : c + 1]
    m0[0, 4:8, :] = jnp.zeros((4, N), F32)
    m0[1] = ph8

    where = [[[place(c, j, d) for d in range(7)] for j in (0, 1)] for c in (0, 1)]
    a_copy.wait()
    stage[0, 0] = a_v[0, 0, where[0][0][SELF]]
    stage[0, 1] = a_v[0, 0, where[0][0][ZM]]
    stage[1, 0] = a_v[1, 1, where[1][1][SELF]]
    stage[1, 1] = a_v[1, 1, where[1][1][ZP]]

    pl.semaphore_wait(barrier, len(FACES) + len(UPWARD))

    far_starts = [
        pltpu.make_async_remote_copy(
            m0, d0.at[opposite(r) // 2 - 3], far_send, far_recv,
            device_id=devices[r], device_id_type=MESH,
        )
        for r in UPWARD
    ]
    for copy in far_starts:
        copy.start()

    def bulk(k, source, target, r):
        return pltpu.make_async_remote_copy(
            source, target, bulk_send.at[k], bulk_recv.at[k],
            device_id=devices[r], device_id_type=MESH,
        )

    sends = [
        bulk(0, p_hbm.at[0, :, 1], pz.at[0], 5),
        bulk(1, p_hbm.at[0, :, 0], pz.at[1], 4),
        bulk(2, p_hbm.at[0], px.at[0], 1),
        bulk(3, p_hbm.at[0], px.at[1], 0),
        bulk(4, p_hbm.at[0, 1], py.at[0], 3),
        bulk(5, p_hbm.at[0, 0], py.at[1], 2),
        bulk(6, stage.at[0], partner.at[0], 4),
        bulk(7, stage.at[1], partner.at[1], 5),
    ]
    near_starts = [
        pltpu.make_async_remote_copy(
            m0, r0.at[opposite(r)], small_send.at[0], small_recv.at[0],
            device_id=devices[r], device_id_type=MESH,
        )
        for r in FACES
    ]
    for k in (2, 3, 0, 1, 6, 7, 4, 5):
        sends[k].start()
    for copy in near_starts:
        copy.start()

    def vector(c, j, d):
        t = 2 * c + j
        if d == SELF:
            block, row = OWN, t
        elif d in (ZM, ZP):
            inner = (d == ZP) == (j == 0)
            block, row = (OWN, 2 * c + 1 - j) if inner else (ZED, t)
        elif d in (XM, XP):
            block, row = 2 + (d - XM), t
        else:
            inner = (d == YP) == (c == 0)
            block, row = (OWN, 2 * (1 - c) + j) if inner else (4 + (d - YM), 2 * (1 - c) + j)
        return w_ref[block, row : row + 1, :]

    def near(c, j, d):
        if d == SELF:
            return p_v[c, j]
        if d in (ZM, ZP):
            inner = (d == ZP) == (j == 0)
            return p_v[c, 1 - j] if inner else pz[0 if d == ZM else 1, c]
        if d in (XM, XP):
            return px[d - XM, c, j]
        inner = (d == YP) == (c == 0)
        return p_v[1 - c, j] if inner else py[d - YM, j]

    def dot(a, b):
        return jnp.dot(a, b, preferred_element_type=F32)

    eye = lax.broadcasted_iota(jnp.int32, (N, N), 0) == lax.broadcasted_iota(
        jnp.int32, (N, N), 1
    )

    def row_sums(block):
        total = jnp.sum(block, axis=1, keepdims=True)
        return jnp.sum(jnp.where(eye, total, 0.0), axis=0, keepdims=True)

    p_copy.wait()
    flipped = [[p_v[c, j].T for j in (0, 1)] for c in (0, 1)]

    def piece(c, j, d):
        block = a_v[c, j, where[c][j][d]]
        result = dot(flipped[c][j], dot(block, near(c, j, d)).astype(BF16))
        t = 2 * c + j
        pieces[t, d] = result
        return result

    INNER_Z = (ZP, ZM)
    OUTER_Z = (ZM, ZP)
    for c in (0, 1):
        for j in (0, 1):
            piece(c, j, SELF)
            piece(c, j, INNER_Z[j])
            acc_a[2 * c + j] = jnp.abs(piece(c, j, YP if c == 0 else YM))

    sends[4].wait_recv()
    sends[5].wait_recv()
    for c in (0, 1):
        d = YM if c == 0 else YP
        for j in (0, 1):
            acc_a[2 * c + j] += jnp.abs(piece(c, j, d))

    sends[0].wait_recv()
    sends[1].wait_recv()
    for c in (0, 1):
        for j in (0, 1):
            piece(c, j, OUTER_Z[j])

    sends[6].wait_recv()
    sends[7].wait_recv()
    for c in (0, 1):
        j = 1 - c
        other = pz[1 - c, c]
        mid_self = dot(partner[c, 0], other).astype(BF16)
        mid_outer = dot(partner[c, 1], p_v[c, j]).astype(BF16)
        turned = other.T
        far = dot(turned, mid_self) + dot(turned, mid_outer)
        t = 2 * c + j
        split = pieces[t, SELF] + pieces[t, OUTER_Z[j]] + far
        whole = (pieces[2 * c, SELF] + pieces[2 * c, ZP]) + (
            pieces[2 * c + 1, SELF] + pieces[2 * c + 1, ZM]
        )
        acc_a[t] += jnp.abs(jnp.where(phase[c] == 1, split, whole))
        for i in (0, 1):
            t = 2 * c + i
            acc_a[t] += jnp.abs(
                jnp.where(phase[c] == 1, pieces[t, INNER_Z[i]], pieces[t, OUTER_Z[i]])
            )

    sends[2].wait_recv()
    sends[3].wait_recv()
    scales = []
    for c in (0, 1):
        for j in (0, 1):
            t = 2 * c + j
            low, high = piece(c, j, XM), piece(c, j, XP)
            scales.append(row_sums(acc_a[t] + jnp.abs(low) + jnp.abs(high)))

    pltpu.make_async_copy(r0, r0, small_recv.at[0]).wait()
    below, above = r0[4, 0, 0:4], r0[5, 0, 0:4]
    mine = m0[0, 0:4]
    w_ref[OWN, 0:4] = jnp.where(straddle4 & even4, below, mine)
    w_ref[ZED, 0:4] = jnp.where(even4, below, jnp.where(straddle4, mine, above))
    pltpu.make_async_copy(d0, d0, far_recv).wait()
    for l in range(4):
        moved = (r0[l, 1, 0:4] > 0.5) & even4
        w_ref[2 + l, 0:4] = jnp.where(moved, d0[l, 0, 0:4], r0[l, 0, 0:4])

    def apply_coarse():
        out = []
        for c in (0, 1):
            for j in (0, 1):
                t = 2 * c + j
                acc = pieces[t, 0] * vector(c, j, 0)
                for d in range(1, 7):
                    acc += pieces[t, d] * vector(c, j, d)
                out.append(row_sums(acc))
        return out

    sums = apply_coarse()
    rhs = rhs_ref[0, :, 0, :]

    def parts(c, lower, upper, extra):
        whole = extra + lower + upper
        split = phase[c] == 1
        return jnp.where(split, lower, whole), jnp.where(split, extra + upper, whole)

    def defects(c, sums):
        return parts(c, -sums[2 * c], -sums[2 * c + 1], rhs[c : c + 1])

    def put(full, swapped, base, pair):
        full[base : base + 1, :] = pair[0]
        full[base + 1 : base + 2, :] = pair[1]
        swapped[base : base + 1, :] = pair[1]
        swapped[base + 1 : base + 2, :] = pair[0]

    def exchange(k, full, swapped, target):
        copies = [
            pltpu.make_async_remote_copy(
                full if r < 4 else swapped, target.at[opposite(r)],
                small_send.at[k], small_recv.at[k],
                device_id=devices[r], device_id_type=MESH,
            )
            for r in ORDER
        ]
        for copy in copies:
            copy.start()
        pltpu.make_async_copy(target, target, small_recv.at[k]).wait()

    def combined(full, target, even, straddle):
        crossing = jnp.where(even, target[4], target[5])
        own = full[...]
        own = own + jnp.where(straddle, crossing, 0.0)
        out = [own, jnp.where(straddle, own, crossing)]
        for l in range(4):
            far = jnp.where(even, target[6 + 2 * l], target[7 + 2 * l])
            moved = r0[l, 1, 0 : even.shape[0]] > 0.5
            out.append(target[l] + jnp.where(moved, far, 0.0))
        return out

    for c in (0, 1):
        put(f1, s1, 2 * c, defects(c, sums))
        put(f1, s1, 4 + 2 * c, parts(c, scales[2 * c], scales[2 * c + 1], EPSILON))
    exchange(1, f1, s1, r1)
    for k, total in enumerate(combined(f1, r1, even8, straddle8)):
        inverse = 1.0 / total[4:8]
        inv_ref[k, 0:4] = inverse
        w_ref[k, 0:4] = w_ref[k, 0:4] + total[0:4] * inverse

    sums = apply_coarse()
    for c in (0, 1):
        put(f2, s2, 2 * c, defects(c, sums))
    exchange(2, f2, s2, r2)
    for k, total in enumerate(combined(f2, r2, even4, straddle4)):
        w_ref[k, 0:4] = w_ref[k, 0:4] + total * inv_ref[k, 0:4]

    sums = apply_coarse()
    last = [defects(c, sums) for c in (0, 1)]
    for c in (0, 1):
        s3[c : c + 1, :] = last[c][0]
    down = pltpu.make_async_remote_copy(
        s3, r3, small_send.at[3], small_recv.at[3], device_id=devices[4], device_id_type=MESH
    )
    down.start()
    for c in (0, 1):
        out_ref[0, c, 0:1, :] = w_ref[OWN, 2 * c + 1 : 2 * c + 2, :]
    down.wait_recv()
    for c in (0, 1):
        out_ref[0, c, 1:2, :] = last[c][1] + jnp.where(phase[c] == 1, r3[c : c + 1, :], 0.0)

    down.wait_send()
    pltpu.make_async_copy(r0, r0, small_send.at[0]).wait()
    pltpu.make_async_copy(d0, d0, far_send).wait()
    pltpu.make_async_copy(r1, r1, small_send.at[1]).wait()
    pltpu.make_async_copy(r2, r2, small_send.at[2]).wait()
    for copy in sends:
        copy.wait_send()


def body(a_blocks, a_cols, p_blocks, agg_ids, coarse_cols, coarse_rhs, coarse_start):
    del coarse_cols
    vmem = pl.BlockSpec(memory_space=pltpu.VMEM)
    hbm = pl.BlockSpec(memory_space=pltpu.HBM)
    one, rows, layers, width = coarse_rhs.shape
    out = pl.pallas_call(
        kernel,
        out_shape=jax.ShapeDtypeStruct((one, rows, 2 * layers, width), F32),
        in_specs=[hbm] * 6,
        out_specs=vmem,
        scratch_shapes=[
            pltpu.SMEM(a_cols.shape, jnp.int32),
            pltpu.SMEM(agg_ids.shape, jnp.int32),
            pltpu.VMEM(coarse_rhs.shape, F32),
            pltpu.VMEM(coarse_start.shape, F32),
            pltpu.VMEM((2, 2, 7, N, N), BF16),
            pltpu.VMEM((2, 2, N, N), BF16),
            pltpu.VMEM((2, 2, 2, N, N), BF16),
            pltpu.VMEM((2, 2, N, N), BF16),
            pltpu.VMEM((2, 2, N, N), BF16),
            pltpu.VMEM((2, 2, N, N), BF16),
            pltpu.VMEM((2, 2, N, N), BF16),
            pltpu.VMEM((4, 7, N, N), F32),
            pltpu.VMEM((4, N, N), F32),
            pltpu.VMEM((6, 8, N), F32),
            pltpu.VMEM((2, 8, N), F32),
            pltpu.VMEM((6, 2, 8, N), F32),
            pltpu.VMEM((4, 2, 8, N), F32),
            pltpu.VMEM((8, N), F32),
            pltpu.VMEM((8, N), F32),
            pltpu.VMEM((14, 8, N), F32),
            pltpu.VMEM((6, 8, N), F32),
            pltpu.VMEM((4, N), F32),
            pltpu.VMEM((4, N), F32),
            pltpu.VMEM((14, 4, N), F32),
            pltpu.VMEM((2, N), F32),
            pltpu.VMEM((2, N), F32),
            pltpu.SemaphoreType.DMA,
            pltpu.SemaphoreType.DMA,
            pltpu.SemaphoreType.DMA((4,)),
            pltpu.SemaphoreType.DMA((8,)),
            pltpu.SemaphoreType.DMA((8,)),
            pltpu.SemaphoreType.DMA((4,)),
            pltpu.SemaphoreType.DMA((4,)),
            pltpu.SemaphoreType.DMA,
            pltpu.SemaphoreType.DMA,
        ],
        compiler_params=pltpu.CompilerParams(
            collective_id=0, has_side_effects=True, vmem_limit_bytes=63 * 2**20
        ),
        name="coarse_setup",
    )(a_blocks, a_cols, p_blocks, agg_ids, coarse_rhs, coarse_start)
    return out[:, :, 0:1], out[:, :, 1:2]


def solution(mesh):
    return jax.shard_map(
        body,
        mesh=mesh,
        in_specs=(
            P("gx", "gy", "gz", None, None, None),
            P("gx", "gy", "gz", None),
            P("gx", "gy", "gz", None, None),
            P("gx", "gy", "gz"),
            P("gx", "gy", "gz", None),
            P("gx", "gy", "gz", None),
            P("gx", "gy", "gz", None),
        ),
        out_specs=(P("gx", "gy", "gz", None), P("gx", "gy", "gz", None)),
        check_vma=False,
    )
```

```python
import jax
import jax.numpy as jnp
from jax import lax
from jax.experimental import pallas as pl
from jax.experimental.pallas import tpu as pltpu
from jax.sharding import PartitionSpec as P

EPSILON = 1e-05
MESH = pl.DeviceIdType.MESH
F32 = jnp.float32
BF16 = jnp.bfloat16
N = 128
SELF, ZM, ZP, XM, XP, YM, YP = range(7)
OWN, ZED = 0, 1
LATERAL = ((-1, 0), (1, 0), (0, -1), (0, 1))
RELATIONS = (
    [(dx, dy, 0) for dx, dy in LATERAL]
    + [(0, 0, -1), (0, 0, 1)]
    + [(dx, dy, dz) for dx, dy in LATERAL for dz in (-1, 1)]
)


def opposite(r):
    return RELATIONS.index(tuple(-d for d in RELATIONS[r]))


FACES = range(6)
UPWARD = (7, 9, 11, 13)
ORDER = list(range(6, 14)) + [4, 5, 0, 1, 2, 3]


def kernel(
    a_hbm, cols_hbm, p_hbm, agg_hbm, rhs_hbm, start_hbm,
    out_ref,
    cols_ref, agg_ref, rhs_ref, start_ref,
    a_v, p_v, px, py, pz, stage, partner, pieces, acc_a,
    w_ref, m0, r0, d0, f1, s1, r1, inv_ref, f2, s2, r2, s3, r3,
    a_sem, p_sem, in_sem, bulk_send, bulk_recv, small_send, small_recv, far_send, far_recv,
):
    gx, gy, gz = lax.axis_index("gx"), lax.axis_index("gy"), lax.axis_index("gz")
    nx, ny, nz = lax.axis_size("gx"), lax.axis_size("gy"), lax.axis_size("gz")
    total_y, total_z = 2 * ny, 2 * nz

    def device(r):
        dx, dy, dz = RELATIONS[r]
        return (
            lax.rem(gx + dx + nx, nx) if dx else gx,
            lax.rem(gy + dy + ny, ny) if dy else gy,
            lax.rem(gz + dz + nz, nz) if dz else gz,
        )

    devices = [device(r) for r in range(14)]
    barrier = pltpu.get_barrier_semaphore()
    for r in (6, 8, 10, 12, *FACES):
        pl.semaphore_signal(barrier, inc=1, device_id=devices[r], device_id_type=MESH)

    inputs = [
        pltpu.make_async_copy(source, target, in_sem.at[k])
        for k, (source, target) in enumerate(
            ((agg_hbm, agg_ref), (start_hbm, start_ref), (cols_hbm, cols_ref), (rhs_hbm, rhs_ref))
        )
    ]
    for copy in inputs:
        copy.start()
    p_copy = pltpu.make_async_copy(p_hbm.at[0], p_v, p_sem)
    p_copy.start()
    a_copy = pltpu.make_async_copy(a_hbm.at[0], a_v, a_sem)
    a_copy.start()

    for copy in inputs:
        copy.wait()

    phase = [
        (agg_ref[0, c, 0] != (gx * total_y + 2 * gy + c) * nz + gz).astype(jnp.int32)
        for c in (0, 1)
    ]

    def place(c, j, d):
        dx = {XM: -1, XP: 1}.get(d, 0)
        dy = {YM: -1, YP: 1}.get(d, 0)
        dz = {ZM: -1, ZP: 1}.get(d, 0)
        x = lax.rem(gx + dx + nx, nx)
        y = lax.rem(2 * gy + c + dy + total_y, total_y)
        z = lax.rem(2 * gz + j + dz + total_z, total_z)
        want = (x * total_y + y) * total_z + z
        found = jnp.int32(0)
        for e in range(1, 7):
            found = jnp.where(cols_ref[0, c, j, e] == want, e, found)
        return found

    row8 = lax.broadcasted_iota(jnp.int32, (8, N), 0)
    even8 = lax.rem(row8, 2) == 0
    even4 = even8[0:4]
    ph8 = jnp.where(lax.rem(row8, 4) < 2, phase[0], phase[1]).astype(F32)
    ph4 = ph8[0:4]
    straddle8 = ph8 > 0.5
    straddle4 = ph4 > 0.5
    start = start_ref[0, :, 0, :]
    for c in (0, 1):
        m0[0, 2 * c : 2 * c + 1, :] = start[c : c + 1]
        m0[0, 2 * c + 1 : 2 * c + 2, :] = start[c : c + 1]
    m0[0, 4:8, :] = jnp.zeros((4, N), F32)
    m0[1] = ph8

    where = [[[place(c, j, d) for d in range(7)] for j in (0, 1)] for c in (0, 1)]
    p_copy.wait()
    a_copy.wait()
    stage[0, 0] = a_v[0, 0, where[0][0][SELF]]
    stage[0, 1] = a_v[0, 0, where[0][0][ZM]]
    stage[1, 0] = a_v[1, 1, where[1][1][SELF]]
    stage[1, 1] = a_v[1, 1, where[1][1][ZP]]

    pl.semaphore_wait(barrier, len(FACES) + len(UPWARD))

    def bulk(k, source, target, r):
        return pltpu.make_async_remote_copy(
            source, target, bulk_send.at[k], bulk_recv.at[k],
            device_id=devices[r], device_id_type=MESH,
        )

    sends = [
        bulk(0, p_v.at[0], px.at[0, 0], 1),
        bulk(1, p_v.at[0], px.at[1, 0], 0),
        bulk(2, p_v.at[1], px.at[0, 1], 1),
        bulk(3, p_v.at[1], px.at[1, 1], 0),
        bulk(4, p_v.at[:, 1], pz.at[0], 5),
        bulk(5, p_v.at[:, 0], pz.at[1], 4),
        bulk(6, stage.at[0], partner.at[0], 4),
        bulk(7, stage.at[1], partner.at[1], 5),
        bulk(8, p_v.at[1], py.at[0], 3),
        bulk(9, p_v.at[0], py.at[1], 2),
    ]
    near_starts = [
        pltpu.make_async_remote_copy(
            m0, r0.at[opposite(r)], small_send.at[0], small_recv.at[0],
            device_id=devices[r], device_id_type=MESH,
        )
        for r in FACES
    ]
    far_starts = [
        pltpu.make_async_remote_copy(
            m0, d0.at[opposite(r) // 2 - 3], far_send, far_recv,
            device_id=devices[r], device_id_type=MESH,
        )
        for r in UPWARD
    ]
    for copy in sends[:4] + far_starts + sends[4:]:
        copy.start()
    for copy in near_starts:
        copy.start()

    def vector(c, j, d):
        t = 2 * c + j
        if d == SELF:
            block, row = OWN, t
        elif d in (ZM, ZP):
            inner = (d == ZP) == (j == 0)
            block, row = (OWN, 2 * c + 1 - j) if inner else (ZED, t)
        elif d in (XM, XP):
            block, row = 2 + (d - XM), t
        else:
            inner = (d == YP) == (c == 0)
            block, row = (OWN, 2 * (1 - c) + j) if inner else (4 + (d - YM), 2 * (1 - c) + j)
        return w_ref[block, row : row + 1, :]

    def near(c, j, d):
        if d == SELF:
            return p_v[c, j]
        if d in (ZM, ZP):
            inner = (d == ZP) == (j == 0)
            return p_v[c, 1 - j] if inner else pz[0 if d == ZM else 1, c]
        if d in (XM, XP):
            return px[d - XM, c, j]
        inner = (d == YP) == (c == 0)
        return p_v[1 - c, j] if inner else py[d - YM, j]

    def dot(a, b):
        return jnp.dot(a, b, preferred_element_type=F32)

    eye = lax.broadcasted_iota(jnp.int32, (N, N), 0) == lax.broadcasted_iota(
        jnp.int32, (N, N), 1
    )

    def row_sums(block):
        total = jnp.sum(block, axis=1, keepdims=True)
        return jnp.sum(jnp.where(eye, total, 0.0), axis=0, keepdims=True)

    flipped = [[p_v[c, j].T for j in (0, 1)] for c in (0, 1)]

    def form(c, j, *directions):
        products = [
            dot(a_v[c, j, where[c][j][d]], near(c, j, d)).astype(BF16) for d in directions
        ]
        joined = dot(flipped[c][j], jnp.concatenate(products, axis=1))
        out = [joined[:, k * N : (k + 1) * N] for k in range(len(directions))]
        for d, result in zip(directions, out):
            pieces[2 * c + j, d] = result
        return out

    INNER_Z, OUTER_Z = (ZP, ZM), (ZM, ZP)
    INNER_Y, OUTER_Y = (YP, YM), (YM, YP)
    for c in (0, 1):
        for j in (0, 1):
            acc_a[2 * c + j] = jnp.abs(form(c, j, SELF, INNER_Z[j], INNER_Y[c])[2])

    for k in (8, 9, 4, 5):
        sends[k].wait_recv()
    for c in (0, 1):
        for j in (0, 1):
            acc_a[2 * c + j] += jnp.abs(form(c, j, OUTER_Z[j], OUTER_Y[c])[1])

    for c in (0, 1):
        sends[2 * c].wait_recv()
        sends[2 * c + 1].wait_recv()
        for j in (0, 1):
            low, high = form(c, j, XM, XP)
            acc_a[2 * c + j] += jnp.abs(low) + jnp.abs(high)

    sends[6].wait_recv()
    sends[7].wait_recv()
    for c in (0, 1):
        j = 1 - c
        other = pz[1 - c, c]
        mid_self = dot(partner[c, 0], other).astype(BF16)
        mid_outer = dot(partner[c, 1], p_v[c, j]).astype(BF16)
        far = dot(
            jnp.concatenate([other.T, other.T], axis=1),
            jnp.concatenate([mid_self, mid_outer], axis=0),
        )
        t = 2 * c + j
        split = pieces[t, SELF] + pieces[t, OUTER_Z[j]] + far
        whole = (pieces[2 * c, SELF] + pieces[2 * c, ZP]) + (
            pieces[2 * c + 1, SELF] + pieces[2 * c + 1, ZM]
        )
        acc_a[t] += jnp.abs(jnp.where(phase[c] == 1, split, whole))
        for i in (0, 1):
            t = 2 * c + i
            acc_a[t] += jnp.abs(
                jnp.where(phase[c] == 1, pieces[t, INNER_Z[i]], pieces[t, OUTER_Z[i]])
            )

    scales = [row_sums(acc_a[t]) for t in range(4)]

    pltpu.make_async_copy(r0, r0, small_recv.at[0]).wait()
    below, above = r0[4, 0, 0:4], r0[5, 0, 0:4]
    mine = m0[0, 0:4]
    w_ref[OWN, 0:4] = jnp.where(straddle4 & even4, below, mine)
    w_ref[ZED, 0:4] = jnp.where(even4, below, jnp.where(straddle4, mine, above))
    pltpu.make_async_copy(d0, d0, far_recv).wait()
    for l in range(4):
        moved = (r0[l, 1, 0:4] > 0.5) & even4
        w_ref[2 + l, 0:4] = jnp.where(moved, d0[l, 0, 0:4], r0[l, 0, 0:4])

    def apply_coarse():
        out = []
        for c in (0, 1):
            for j in (0, 1):
                t = 2 * c + j
                acc = pieces[t, 0] * vector(c, j, 0)
                for d in range(1, 7):
                    acc += pieces[t, d] * vector(c, j, d)
                out.append(row_sums(acc))
        return out

    sums = apply_coarse()
    rhs = rhs_ref[0, :, 0, :]

    def parts(c, lower, upper, extra):
        whole = extra + lower + upper
        split = phase[c] == 1
        return jnp.where(split, lower, whole), jnp.where(split, extra + upper, whole)

    def defects(c, sums):
        return parts(c, -sums[2 * c], -sums[2 * c + 1], rhs[c : c + 1])

    def put(full, swapped, base, pair):
        full[base : base + 1, :] = pair[0]
        full[base + 1 : base + 2, :] = pair[1]
        swapped[base : base + 1, :] = pair[1]
        swapped[base + 1 : base + 2, :] = pair[0]

    def exchange(k, full, swapped, target):
        copies = [
            pltpu.make_async_remote_copy(
                full if r < 4 else swapped, target.at[opposite(r)],
                small_send.at[k], small_recv.at[k],
                device_id=devices[r], device_id_type=MESH,
            )
            for r in ORDER
        ]
        for copy in copies:
            copy.start()
        pltpu.make_async_copy(target, target, small_recv.at[k]).wait()

    def combined(full, target, even, straddle):
        crossing = jnp.where(even, target[4], target[5])
        own = full[...]
        own = own + jnp.where(straddle, crossing, 0.0)
        out = [own, jnp.where(straddle, own, crossing)]
        for l in range(4):
            far = jnp.where(even, target[6 + 2 * l], target[7 + 2 * l])
            moved = r0[l, 1, 0 : even.shape[0]] > 0.5
            out.append(target[l] + jnp.where(moved, far, 0.0))
        return out

    for c in (0, 1):
        put(f1, s1, 2 * c, defects(c, sums))
        put(f1, s1, 4 + 2 * c, parts(c, scales[2 * c], scales[2 * c + 1], EPSILON))
    exchange(1, f1, s1, r1)
    for k, total in enumerate(combined(f1, r1, even8, straddle8)):
        inverse = 1.0 / total[4:8]
        inv_ref[k, 0:4] = inverse
        w_ref[k, 0:4] = w_ref[k, 0:4] + total[0:4] * inverse

    sums = apply_coarse()
    for c in (0, 1):
        put(f2, s2, 2 * c, defects(c, sums))
    exchange(2, f2, s2, r2)
    for k, total in enumerate(combined(f2, r2, even4, straddle4)):
        w_ref[k, 0:4] = w_ref[k, 0:4] + total * inv_ref[k, 0:4]

    sums = apply_coarse()
    last = [defects(c, sums) for c in (0, 1)]
    for c in (0, 1):
        s3[c : c + 1, :] = last[c][0]
    down = pltpu.make_async_remote_copy(
        s3, r3, small_send.at[3], small_recv.at[3], device_id=devices[4], device_id_type=MESH
    )
    down.start()
    for c in (0, 1):
        out_ref[0, c, 0:1, :] = w_ref[OWN, 2 * c + 1 : 2 * c + 2, :]
    down.wait_recv()
    for c in (0, 1):
        out_ref[0, c, 1:2, :] = last[c][1] + jnp.where(phase[c] == 1, r3[c : c + 1, :], 0.0)

    down.wait_send()
    pltpu.make_async_copy(r0, r0, small_send.at[0]).wait()
    pltpu.make_async_copy(d0, d0, far_send).wait()
    pltpu.make_async_copy(r1, r1, small_send.at[1]).wait()
    pltpu.make_async_copy(r2, r2, small_send.at[2]).wait()
    for copy in sends:
        copy.wait_send()


def body(a_blocks, a_cols, p_blocks, agg_ids, coarse_cols, coarse_rhs, coarse_start):
    del coarse_cols
    vmem = pl.BlockSpec(memory_space=pltpu.VMEM)
    hbm = pl.BlockSpec(memory_space=pltpu.HBM)
    one, rows, layers, width = coarse_rhs.shape
    out = pl.pallas_call(
        kernel,
        out_shape=pltpu.VMEM((one, rows, 2 * layers, width), F32),
        in_specs=[hbm] * 6,
        out_specs=vmem,
        scratch_shapes=[
            pltpu.SMEM(a_cols.shape, jnp.int32),
            pltpu.SMEM(agg_ids.shape, jnp.int32),
            pltpu.VMEM(coarse_rhs.shape, F32),
            pltpu.VMEM(coarse_start.shape, F32),
            pltpu.VMEM((2, 2, 7, N, N), BF16),
            pltpu.VMEM((2, 2, N, N), BF16),
            pltpu.VMEM((2, 2, 2, N, N), BF16),
            pltpu.VMEM((2, 2, N, N), BF16),
            pltpu.VMEM((2, 2, N, N), BF16),
            pltpu.VMEM((2, 2, N, N), BF16),
            pltpu.VMEM((2, 2, N, N), BF16),
            pltpu.VMEM((4, 7, N, N), F32),
            pltpu.VMEM((4, N, N), F32),
            pltpu.VMEM((6, 8, N), F32),
            pltpu.VMEM((2, 8, N), F32),
            pltpu.VMEM((6, 2, 8, N), F32),
            pltpu.VMEM((4, 2, 8, N), F32),
            pltpu.VMEM((8, N), F32),
            pltpu.VMEM((8, N), F32),
            pltpu.VMEM((14, 8, N), F32),
            pltpu.VMEM((6, 8, N), F32),
            pltpu.VMEM((4, N), F32),
            pltpu.VMEM((4, N), F32),
            pltpu.VMEM((14, 4, N), F32),
            pltpu.VMEM((2, N), F32),
            pltpu.VMEM((2, N), F32),
            pltpu.SemaphoreType.DMA,
            pltpu.SemaphoreType.DMA,
            pltpu.SemaphoreType.DMA((4,)),
            pltpu.SemaphoreType.DMA((10,)),
            pltpu.SemaphoreType.DMA((10,)),
            pltpu.SemaphoreType.DMA((4,)),
            pltpu.SemaphoreType.DMA((4,)),
            pltpu.SemaphoreType.DMA,
            pltpu.SemaphoreType.DMA,
        ],
        compiler_params=pltpu.CompilerParams(
            collective_id=0, has_side_effects=True, vmem_limit_bytes=63 * 2**20
        ),
        name="coarse_setup",
    )(a_blocks, a_cols, p_blocks, agg_ids, coarse_rhs, coarse_start)
    return out[:, :, 0:1], out[:, :, 1:2]


def solution(mesh):
    return jax.shard_map(
        body,
        mesh=mesh,
        in_specs=(
            P("gx", "gy", "gz", None, None, None),
            P("gx", "gy", "gz", None),
            P("gx", "gy", "gz", None, None),
            P("gx", "gy", "gz"),
            P("gx", "gy", "gz", None),
            P("gx", "gy", "gz", None),
            P("gx", "gy", "gz", None),
        ),
        out_specs=(P("gx", "gy", "gz", None), P("gx", "gy", "gz", None)),
        check_vma=False,
    )
```

```python
import jax
import jax.numpy as jnp
from jax import lax
from jax.experimental import pallas as pl
from jax.experimental.pallas import tpu as pltpu
from jax.sharding import PartitionSpec as P

EPSILON = 1e-05
MESH = pl.DeviceIdType.MESH
F32 = jnp.float32
BF16 = jnp.bfloat16
N = 128
SELF, ZM, ZP, XM, XP, YM, YP = range(7)
OWN, ZED = 0, 1
LATERAL = ((-1, 0), (1, 0), (0, -1), (0, 1))
RELATIONS = (
    [(dx, dy, 0) for dx, dy in LATERAL]
    + [(0, 0, -1), (0, 0, 1)]
    + [(dx, dy, dz) for dx, dy in LATERAL for dz in (-1, 1)]
)


def opposite(r):
    return RELATIONS.index(tuple(-d for d in RELATIONS[r]))


FACES = range(6)
UPWARD = (7, 9, 11, 13)
ORDER = list(range(6, 14)) + [4, 5, 0, 1, 2, 3]


def kernel(
    a_hbm, cols_hbm, p_hbm, agg_hbm, rhs_hbm, start_hbm,
    out_ref,
    cols_ref, agg_ref, rhs_ref, start_ref,
    a_v, p_v, px, py, pz, stage, partner, pieces, acc_a, acc_y, ahead,
    w_ref, m0, r0, d0, f1, s1, r1, inv_ref, f2, s2, r2, s3, r3,
    a_sem, p_sem, in_sem, bulk_send, bulk_recv, small_send, side_recv, z_recv, far_send, far_recv, last_recv,
):
    gx, gy, gz = lax.axis_index("gx"), lax.axis_index("gy"), lax.axis_index("gz")
    nx, ny, nz = lax.axis_size("gx"), lax.axis_size("gy"), lax.axis_size("gz")
    total_y, total_z = 2 * ny, 2 * nz

    def device(r):
        dx, dy, dz = RELATIONS[r]
        return (
            lax.rem(gx + dx + nx, nx) if dx else gx,
            lax.rem(gy + dy + ny, ny) if dy else gy,
            lax.rem(gz + dz + nz, nz) if dz else gz,
        )

    devices = [device(r) for r in range(14)]
    barrier = pltpu.get_barrier_semaphore()
    for r in (6, 8, 10, 12, *FACES):
        pl.semaphore_signal(barrier, inc=1, device_id=devices[r], device_id_type=MESH)

    inputs = [
        pltpu.make_async_copy(source, target, in_sem.at[k])
        for k, (source, target) in enumerate(
            ((agg_hbm, agg_ref), (start_hbm, start_ref), (cols_hbm, cols_ref), (rhs_hbm, rhs_ref))
        )
    ]
    for copy in inputs:
        copy.start()
    p_copy = pltpu.make_async_copy(p_hbm.at[0], p_v, p_sem)
    p_copy.start()
    a_copy = pltpu.make_async_copy(a_hbm.at[0], a_v, a_sem)
    a_copy.start()

    for copy in inputs:
        copy.wait()

    phase = [
        (agg_ref[0, c, 0] != (gx * total_y + 2 * gy + c) * nz + gz).astype(jnp.int32)
        for c in (0, 1)
    ]

    def place(c, j, d):
        dx = {XM: -1, XP: 1}.get(d, 0)
        dy = {YM: -1, YP: 1}.get(d, 0)
        dz = {ZM: -1, ZP: 1}.get(d, 0)
        x = lax.rem(gx + dx + nx, nx)
        y = lax.rem(2 * gy + c + dy + total_y, total_y)
        z = lax.rem(2 * gz + j + dz + total_z, total_z)
        want = (x * total_y + y) * total_z + z
        found = jnp.int32(0)
        for e in range(1, 7):
            found = jnp.where(cols_ref[0, c, j, e] == want, e, found)
        return found

    row8 = lax.broadcasted_iota(jnp.int32, (8, N), 0)
    even8 = lax.rem(row8, 2) == 0
    even4 = even8[0:4]
    ph8 = jnp.where(lax.rem(row8, 4) < 2, phase[0], phase[1]).astype(F32)
    ph4 = ph8[0:4]
    straddle8 = ph8 > 0.5
    straddle4 = ph4 > 0.5
    start = start_ref[0, :, 0, :]
    for c in (0, 1):
        m0[0, 2 * c : 2 * c + 1, :] = start[c : c + 1]
        m0[0, 2 * c + 1 : 2 * c + 2, :] = start[c : c + 1]
    m0[0, 4:8, :] = jnp.zeros((4, N), F32)
    m0[1] = ph8

    where = [[[place(c, j, d) for d in range(7)] for j in (0, 1)] for c in (0, 1)]
    p_copy.wait()
    a_copy.wait()
    stage[0, 0] = a_v[0, 0, where[0][0][SELF]]
    stage[0, 1] = a_v[0, 0, where[0][0][ZM]]
    stage[1, 0] = a_v[1, 1, where[1][1][SELF]]
    stage[1, 1] = a_v[1, 1, where[1][1][ZP]]

    pl.semaphore_wait(barrier, len(FACES) + len(UPWARD))

    def arrival(k, r):
        return (side_recv if r < 4 else z_recv if r < 6 else far_recv).at[k]

    def await_arrival(buffer, semaphore):
        pltpu.make_async_copy(buffer, buffer, semaphore).wait()

    def bulk(k, source, target, r):
        return pltpu.make_async_remote_copy(
            source, target, bulk_send.at[k], bulk_recv.at[k],
            device_id=devices[r], device_id_type=MESH,
        )

    sends = [
        bulk(0, p_v.at[0], px.at[0, 0], 1),
        bulk(1, p_v.at[0], px.at[1, 0], 0),
        bulk(2, p_v.at[1], px.at[0, 1], 1),
        bulk(3, p_v.at[1], px.at[1, 1], 0),
        bulk(4, p_v.at[:, 1], pz.at[0], 5),
        bulk(5, p_v.at[:, 0], pz.at[1], 4),
        bulk(6, stage.at[0], partner.at[0], 4),
        bulk(7, stage.at[1], partner.at[1], 5),
        bulk(8, p_v.at[1], py.at[0], 3),
        bulk(9, p_v.at[0], py.at[1], 2),
    ]
    near_starts = [
        pltpu.make_async_remote_copy(
            m0, r0.at[opposite(r)], small_send.at[0], arrival(0, r),
            device_id=devices[r], device_id_type=MESH,
        )
        for r in FACES
    ]
    far_starts = [
        pltpu.make_async_remote_copy(
            m0, d0.at[opposite(r) // 2 - 3], far_send, far_recv.at[0],
            device_id=devices[r], device_id_type=MESH,
        )
        for r in UPWARD
    ]
    for copy in sends[:4] + far_starts + sends[4:6] + near_starts[4:] + sends[6:]:
        copy.start()
    for copy in near_starts[:4]:
        copy.start()

    def vector(c, j, d):
        t = 2 * c + j
        if d == SELF:
            block, row = OWN, t
        elif d in (ZM, ZP):
            inner = (d == ZP) == (j == 0)
            block, row = (OWN, 2 * c + 1 - j) if inner else (ZED, t)
        elif d in (XM, XP):
            block, row = 2 + (d - XM), t
        else:
            inner = (d == YP) == (c == 0)
            block, row = (OWN, 2 * (1 - c) + j) if inner else (4 + (d - YM), 2 * (1 - c) + j)
        return w_ref[block, row : row + 1, :]

    def near(c, j, d):
        if d == SELF:
            return p_v[c, j]
        if d in (ZM, ZP):
            inner = (d == ZP) == (j == 0)
            return p_v[c, 1 - j] if inner else pz[0 if d == ZM else 1, c]
        if d in (XM, XP):
            return px[d - XM, c, j]
        inner = (d == YP) == (c == 0)
        return p_v[1 - c, j] if inner else py[d - YM, j]

    def dot(a, b):
        return jnp.dot(a, b, preferred_element_type=F32)

    eye = lax.broadcasted_iota(jnp.int32, (N, N), 0) == lax.broadcasted_iota(
        jnp.int32, (N, N), 1
    )

    def row_sums(block):
        total = jnp.sum(block, axis=1, keepdims=True)
        return jnp.sum(jnp.where(eye, total, 0.0), axis=0, keepdims=True)

    flipped = [[p_v[c, j].T for j in (0, 1)] for c in (0, 1)]

    INNER_Z, OUTER_Z = (ZP, ZM), (ZM, ZP)
    INNER_Y, OUTER_Y = (YP, YM), (YM, YP)

    def form(c, j, *directions):
        products = [
            dot(a_v[c, j, where[c][j][d]], near(c, j, d)).astype(BF16) for d in directions
        ]
        joined = dot(flipped[c][j], jnp.concatenate(products, axis=1))
        out = [joined[:, k * N : (k + 1) * N] for k in range(len(directions))]
        for d, result in zip(directions, out):
            pieces[2 * c + j, d] = result
        return out

    def outer(c, j):
        return (OUTER_Z[j], OUTER_Y[c], XM, XP)

    def prepare(c, j):
        for k, d in enumerate(outer(c, j)):
            left = dot(flipped[c][j], a_v[c, j, where[c][j][d]])
            lead = left.astype(BF16)
            ahead[2 * c + j, k, :, :N] = lead
            ahead[2 * c + j, k, :, N:] = (left - lead.astype(F32)).astype(BF16)

    def finish(c, j, d):
        block = near(c, j, d)
        result = dot(ahead[2 * c + j, outer(c, j).index(d)], jnp.concatenate([block, block], axis=0))
        pieces[2 * c + j, d] = result
        return result

    def add_up(c, j, directions):
        t = 2 * c + j
        acc = pieces[t, directions[0]] * vector(c, j, directions[0])
        for d in directions[1:]:
            acc += pieces[t, d] * vector(c, j, d)
        return acc

    def apply_here():
        for c in (0, 1):
            for j in (0, 1):
                acc_y[2 * c + j] = add_up(c, j, (SELF, ZM, ZP, INNER_Y[c]))

    def apply_rest():
        return [
            row_sums(acc_y[2 * c + j] + add_up(c, j, (OUTER_Y[c], XM, XP)))
            for c in (0, 1)
            for j in (0, 1)
        ]

    for c in (0, 1):
        for j in (0, 1):
            acc_a[2 * c + j] = jnp.abs(form(c, j, SELF, INNER_Z[j], INNER_Y[c])[2])
            prepare(c, j)

    for k in (8, 9, 4, 5):
        sends[k].wait_recv()
    for c in (0, 1):
        for j in (0, 1):
            finish(c, j, OUTER_Z[j])
            acc_a[2 * c + j] += jnp.abs(finish(c, j, OUTER_Y[c]))

    await_arrival(r0.at[4:6], z_recv.at[0])
    below, above = r0[4, 0, 0:4], r0[5, 0, 0:4]
    mine = m0[0, 0:4]
    w_ref[OWN, 0:4] = jnp.where(straddle4 & even4, below, mine)
    w_ref[ZED, 0:4] = jnp.where(even4, below, jnp.where(straddle4, mine, above))
    apply_here()

    for c in (0, 1):
        sends[2 * c].wait_recv()
        sends[2 * c + 1].wait_recv()
        for j in (0, 1):
            acc_a[2 * c + j] += jnp.abs(finish(c, j, XM)) + jnp.abs(finish(c, j, XP))

    sends[6].wait_recv()
    sends[7].wait_recv()
    for c in (0, 1):
        j = 1 - c
        other = pz[1 - c, c]
        mid_self = dot(partner[c, 0], other).astype(BF16)
        mid_outer = dot(partner[c, 1], p_v[c, j]).astype(BF16)
        far = dot(
            jnp.concatenate([other.T, other.T], axis=1),
            jnp.concatenate([mid_self, mid_outer], axis=0),
        )
        t = 2 * c + j
        split = pieces[t, SELF] + pieces[t, OUTER_Z[j]] + far
        whole = (pieces[2 * c, SELF] + pieces[2 * c, ZP]) + (
            pieces[2 * c + 1, SELF] + pieces[2 * c + 1, ZM]
        )
        acc_a[t] += jnp.abs(jnp.where(phase[c] == 1, split, whole))
        for i in (0, 1):
            t = 2 * c + i
            acc_a[t] += jnp.abs(
                jnp.where(phase[c] == 1, pieces[t, INNER_Z[i]], pieces[t, OUTER_Z[i]])
            )

    scales = [row_sums(acc_a[t]) for t in range(4)]

    await_arrival(r0.at[0:4], side_recv.at[0])
    await_arrival(d0, far_recv.at[0])
    for l in range(4):
        moved = (r0[l, 1, 0:4] > 0.5) & even4
        w_ref[2 + l, 0:4] = jnp.where(moved, d0[l, 0, 0:4], r0[l, 0, 0:4])
    sums = apply_rest()

    rhs = rhs_ref[0, :, 0, :]

    def parts(c, lower, upper, extra):
        whole = extra + lower + upper
        split = phase[c] == 1
        return jnp.where(split, lower, whole), jnp.where(split, extra + upper, whole)

    def defects(c, sums):
        return parts(c, -sums[2 * c], -sums[2 * c + 1], rhs[c : c + 1])

    def put(full, swapped, base, pair):
        full[base : base + 1, :] = pair[0]
        full[base + 1 : base + 2, :] = pair[1]
        swapped[base : base + 1, :] = pair[1]
        swapped[base + 1 : base + 2, :] = pair[0]

    def exchange(k, full, swapped, target):
        copies = [
            pltpu.make_async_remote_copy(
                full if r < 4 else swapped, target.at[opposite(r)],
                small_send.at[k], arrival(k, r),
                device_id=devices[r], device_id_type=MESH,
            )
            for r in ORDER
        ]
        for copy in copies:
            copy.start()

    def combined_here(k, full, target, even, straddle):
        await_arrival(target.at[4:6], z_recv.at[k])
        crossing = jnp.where(even, target[4], target[5])
        own = full[...] + jnp.where(straddle, crossing, 0.0)
        return [own, jnp.where(straddle, own, crossing)]

    def combined_rest(k, target, even):
        await_arrival(target.at[0:4], side_recv.at[k])
        await_arrival(target.at[6:14], far_recv.at[k])
        out = []
        for l in range(4):
            far = jnp.where(even, target[6 + 2 * l], target[7 + 2 * l])
            moved = r0[l, 1, 0 : even.shape[0]] > 0.5
            out.append(target[l] + jnp.where(moved, far, 0.0))
        return out

    def first_step(k, total):
        inverse = 1.0 / total[4:8]
        inv_ref[k, 0:4] = inverse
        w_ref[k, 0:4] = w_ref[k, 0:4] + total[0:4] * inverse

    def next_step(k, total):
        w_ref[k, 0:4] = w_ref[k, 0:4] + total * inv_ref[k, 0:4]

    for c in (0, 1):
        put(f1, s1, 2 * c, defects(c, sums))
        put(f1, s1, 4 + 2 * c, parts(c, scales[2 * c], scales[2 * c + 1], EPSILON))
    exchange(1, f1, s1, r1)
    await_arrival(r0, small_send.at[0])
    await_arrival(d0, far_send)
    for copy in sends:
        copy.wait_send()
    for k, total in enumerate(combined_here(1, f1, r1, even8, straddle8)):
        first_step(k, total)
    apply_here()
    for k, total in enumerate(combined_rest(1, r1, even8)):
        first_step(2 + k, total)
    sums = apply_rest()

    for c in (0, 1):
        put(f2, s2, 2 * c, defects(c, sums))
    exchange(2, f2, s2, r2)
    await_arrival(r1, small_send.at[1])
    for k, total in enumerate(combined_here(2, f2, r2, even4, straddle4)):
        next_step(k, total)
    apply_here()
    for k, total in enumerate(combined_rest(2, r2, even4)):
        next_step(2 + k, total)
    sums = apply_rest()

    last = [defects(c, sums) for c in (0, 1)]
    for c in (0, 1):
        s3[c : c + 1, :] = last[c][0]
    down = pltpu.make_async_remote_copy(
        s3, r3, small_send.at[3], last_recv, device_id=devices[4], device_id_type=MESH
    )
    down.start()
    await_arrival(r2, small_send.at[2])
    for c in (0, 1):
        out_ref[0, c, 0:1, :] = w_ref[OWN, 2 * c + 1 : 2 * c + 2, :]
    down.wait_recv()
    for c in (0, 1):
        out_ref[0, c, 1:2, :] = last[c][1] + jnp.where(phase[c] == 1, r3[c : c + 1, :], 0.0)

    down.wait_send()


def body(a_blocks, a_cols, p_blocks, agg_ids, coarse_cols, coarse_rhs, coarse_start):
    del coarse_cols
    vmem = pl.BlockSpec(memory_space=pltpu.VMEM)
    hbm = pl.BlockSpec(memory_space=pltpu.HBM)
    one, rows, layers, width = coarse_rhs.shape
    out = pl.pallas_call(
        kernel,
        out_shape=pltpu.VMEM((one, rows, 2 * layers, width), F32),
        in_specs=[hbm] * 6,
        out_specs=vmem,
        scratch_shapes=[
            pltpu.SMEM(a_cols.shape, jnp.int32),
            pltpu.SMEM(agg_ids.shape, jnp.int32),
            pltpu.VMEM(coarse_rhs.shape, F32),
            pltpu.VMEM(coarse_start.shape, F32),
            pltpu.VMEM((2, 2, 7, N, N), BF16),
            pltpu.VMEM((2, 2, N, N), BF16),
            pltpu.VMEM((2, 2, 2, N, N), BF16),
            pltpu.VMEM((2, 2, N, N), BF16),
            pltpu.VMEM((2, 2, N, N), BF16),
            pltpu.VMEM((2, 2, N, N), BF16),
            pltpu.VMEM((2, 2, N, N), BF16),
            pltpu.VMEM((4, 7, N, N), F32),
            pltpu.VMEM((4, N, N), F32),
            pltpu.VMEM((4, N, N), F32),
            pltpu.VMEM((4, 4, N, 2 * N), BF16),
            pltpu.VMEM((6, 8, N), F32),
            pltpu.VMEM((2, 8, N), F32),
            pltpu.VMEM((6, 2, 8, N), F32),
            pltpu.VMEM((4, 2, 8, N), F32),
            pltpu.VMEM((8, N), F32),
            pltpu.VMEM((8, N), F32),
            pltpu.VMEM((14, 8, N), F32),
            pltpu.VMEM((6, 8, N), F32),
            pltpu.VMEM((4, N), F32),
            pltpu.VMEM((4, N), F32),
            pltpu.VMEM((14, 4, N), F32),
            pltpu.VMEM((2, N), F32),
            pltpu.VMEM((2, N), F32),
            pltpu.SemaphoreType.DMA,
            pltpu.SemaphoreType.DMA,
            pltpu.SemaphoreType.DMA((4,)),
            pltpu.SemaphoreType.DMA((10,)),
            pltpu.SemaphoreType.DMA((10,)),
            pltpu.SemaphoreType.DMA((4,)),
            pltpu.SemaphoreType.DMA((3,)),
            pltpu.SemaphoreType.DMA((3,)),
            pltpu.SemaphoreType.DMA,
            pltpu.SemaphoreType.DMA((3,)),
            pltpu.SemaphoreType.DMA,
        ],
        compiler_params=pltpu.CompilerParams(
            collective_id=0, has_side_effects=True, vmem_limit_bytes=63 * 2**20
        ),
        name="coarse_setup",
    )(a_blocks, a_cols, p_blocks, agg_ids, coarse_rhs, coarse_start)
    return out[:, :, 0:1], out[:, :, 1:2]


def solution(mesh):
    return jax.shard_map(
        body,
        mesh=mesh,
        in_specs=(
            P("gx", "gy", "gz", None, None, None),
            P("gx", "gy", "gz", None),
            P("gx", "gy", "gz", None, None),
            P("gx", "gy", "gz"),
            P("gx", "gy", "gz", None),
            P("gx", "gy", "gz", None),
            P("gx", "gy", "gz", None),
        ),
        out_specs=(P("gx", "gy", "gz", None), P("gx", "gy", "gz", None)),
        check_vma=False,
    )
```

```python
import jax
import jax.numpy as jnp
from jax import lax
from jax.experimental import pallas as pl
from jax.experimental.pallas import tpu as pltpu
from jax.sharding import PartitionSpec as P

EPSILON = 1e-05
MESH = pl.DeviceIdType.MESH
F32 = jnp.float32
BF16 = jnp.bfloat16
N = 128
SELF, ZM, ZP, XM, XP, YM, YP = range(7)
OWN, ZED = 0, 1
LATERAL = ((-1, 0), (1, 0), (0, -1), (0, 1))
RELATIONS = (
    [(dx, dy, 0) for dx, dy in LATERAL]
    + [(0, 0, -1), (0, 0, 1)]
    + [(dx, dy, dz) for dx, dy in LATERAL for dz in (-1, 1)]
)


def opposite(r):
    return RELATIONS.index(tuple(-d for d in RELATIONS[r]))


FACES = range(6)
UPWARD = (7, 9, 11, 13)
ORDER = list(range(6, 14)) + [4, 5, 0, 1, 2, 3]


def kernel(
    a_hbm, cols_hbm, p_hbm, agg_hbm, rhs_hbm, start_hbm,
    out_ref,
    cols_ref, agg_ref, rhs_ref, start_ref,
    a_v, p_v, px, py, pz, stage, partner, pieces, acc_a, acc_y, ahead,
    w_ref, m0, r0, d0, f1, s1, r1, inv_ref, f2, s2, r2, s3, r3,
    a_sem, p_sem, in_sem, bulk_send, bulk_recv, small_send, side_recv, z_recv, far_send, far_recv, last_recv,
):
    gx, gy, gz = lax.axis_index("gx"), lax.axis_index("gy"), lax.axis_index("gz")
    nx, ny, nz = lax.axis_size("gx"), lax.axis_size("gy"), lax.axis_size("gz")
    total_y, total_z = 2 * ny, 2 * nz

    def device(r):
        dx, dy, dz = RELATIONS[r]
        return (
            lax.rem(gx + dx + nx, nx) if dx else gx,
            lax.rem(gy + dy + ny, ny) if dy else gy,
            lax.rem(gz + dz + nz, nz) if dz else gz,
        )

    devices = [device(r) for r in range(14)]
    barrier = pltpu.get_barrier_semaphore()
    for r in (6, 8, 10, 12, *FACES):
        pl.semaphore_signal(barrier, inc=1, device_id=devices[r], device_id_type=MESH)

    inputs = [
        pltpu.make_async_copy(source, target, in_sem.at[k])
        for k, (source, target) in enumerate(
            ((agg_hbm, agg_ref), (start_hbm, start_ref), (cols_hbm, cols_ref), (rhs_hbm, rhs_ref))
        )
    ]
    for copy in inputs:
        copy.start()
    p_copy = pltpu.make_async_copy(p_hbm.at[0], p_v, p_sem)
    p_copy.start()
    a_copy = pltpu.make_async_copy(a_hbm.at[0], a_v, a_sem)
    a_copy.start()

    for copy in inputs:
        copy.wait()

    phase = [
        (agg_ref[0, c, 0] != (gx * total_y + 2 * gy + c) * nz + gz).astype(jnp.int32)
        for c in (0, 1)
    ]

    def place(c, j, d):
        dx = {XM: -1, XP: 1}.get(d, 0)
        dy = {YM: -1, YP: 1}.get(d, 0)
        dz = {ZM: -1, ZP: 1}.get(d, 0)
        x = lax.rem(gx + dx + nx, nx)
        y = lax.rem(2 * gy + c + dy + total_y, total_y)
        z = lax.rem(2 * gz + j + dz + total_z, total_z)
        want = (x * total_y + y) * total_z + z
        found = jnp.int32(0)
        for e in range(1, 7):
            found = jnp.where(cols_ref[0, c, j, e] == want, e, found)
        return found

    row8 = lax.broadcasted_iota(jnp.int32, (8, N), 0)
    even8 = lax.rem(row8, 2) == 0
    even4 = even8[0:4]
    ph8 = jnp.where(lax.rem(row8, 4) < 2, phase[0], phase[1]).astype(F32)
    ph4 = ph8[0:4]
    straddle8 = ph8 > 0.5
    straddle4 = ph4 > 0.5
    start = start_ref[0, :, 0, :]
    for c in (0, 1):
        m0[0, 2 * c : 2 * c + 1, :] = start[c : c + 1]
        m0[0, 2 * c + 1 : 2 * c + 2, :] = start[c : c + 1]
    m0[0, 4:8, :] = jnp.zeros((4, N), F32)
    m0[1] = ph8

    where = [[[place(c, j, d) for d in range(7)] for j in (0, 1)] for c in (0, 1)]
    p_copy.wait()
    a_copy.wait()
    stage[0, 0] = a_v[0, 0, where[0][0][SELF]]
    stage[0, 1] = a_v[0, 0, where[0][0][ZM]]
    stage[1, 0] = a_v[1, 1, where[1][1][SELF]]
    stage[1, 1] = a_v[1, 1, where[1][1][ZP]]

    pl.semaphore_wait(barrier, len(FACES) + len(UPWARD))

    def arrival(k, r):
        return (side_recv if r < 4 else z_recv if r < 6 else far_recv).at[k]

    def await_arrival(buffer, semaphore):
        pltpu.make_async_copy(buffer, buffer, semaphore).wait()

    def bulk(k, source, target, r):
        return pltpu.make_async_remote_copy(
            source, target, bulk_send.at[k], bulk_recv.at[k],
            device_id=devices[r], device_id_type=MESH,
        )

    sends = [
        bulk(0, p_v.at[0], px.at[0, 0], 1),
        bulk(1, p_v.at[0], px.at[1, 0], 0),
        bulk(2, p_v.at[1], px.at[0, 1], 1),
        bulk(3, p_v.at[1], px.at[1, 1], 0),
        bulk(4, p_v.at[:, 1], pz.at[0], 5),
        bulk(5, p_v.at[:, 0], pz.at[1], 4),
        bulk(6, stage.at[0], partner.at[0], 4),
        bulk(7, stage.at[1], partner.at[1], 5),
        bulk(8, p_v.at[1], py.at[0], 3),
        bulk(9, p_v.at[0], py.at[1], 2),
    ]
    near_starts = [
        pltpu.make_async_remote_copy(
            m0, r0.at[opposite(r)], small_send.at[0], arrival(0, r),
            device_id=devices[r], device_id_type=MESH,
        )
        for r in FACES
    ]
    far_starts = [
        pltpu.make_async_remote_copy(
            m0, d0.at[opposite(r) // 2 - 3], far_send, far_recv.at[0],
            device_id=devices[r], device_id_type=MESH,
        )
        for r in UPWARD
    ]
    for copy in sends[:4] + far_starts + sends[4:6] + near_starts[4:] + sends[8:] + sends[6:8] + near_starts[:4]:
        copy.start()

    def vector(c, j, d):
        t = 2 * c + j
        if d == SELF:
            block, row = OWN, t
        elif d in (ZM, ZP):
            inner = (d == ZP) == (j == 0)
            block, row = (OWN, 2 * c + 1 - j) if inner else (ZED, t)
        elif d in (XM, XP):
            block, row = 2 + (d - XM), t
        else:
            inner = (d == YP) == (c == 0)
            block, row = (OWN, 2 * (1 - c) + j) if inner else (4 + (d - YM), 2 * (1 - c) + j)
        return w_ref[block, row : row + 1, :]

    def near(c, j, d):
        if d == SELF:
            return p_v[c, j]
        if d in (ZM, ZP):
            inner = (d == ZP) == (j == 0)
            return p_v[c, 1 - j] if inner else pz[0 if d == ZM else 1, c]
        if d in (XM, XP):
            return px[d - XM, c, j]
        inner = (d == YP) == (c == 0)
        return p_v[1 - c, j] if inner else py[d - YM, j]

    def dot(a, b):
        return jnp.dot(a, b, preferred_element_type=F32)

    eye = lax.broadcasted_iota(jnp.int32, (N, N), 0) == lax.broadcasted_iota(
        jnp.int32, (N, N), 1
    )

    def row_sums(block):
        total = jnp.sum(block, axis=1, keepdims=True)
        return jnp.sum(jnp.where(eye, total, 0.0), axis=0, keepdims=True)

    flipped = [[p_v[c, j].T for j in (0, 1)] for c in (0, 1)]

    INNER_Z, OUTER_Z = (ZP, ZM), (ZM, ZP)
    INNER_Y, OUTER_Y = (YP, YM), (YM, YP)

    def form(c, j, *directions):
        products = [
            dot(a_v[c, j, where[c][j][d]], near(c, j, d)).astype(BF16) for d in directions
        ]
        joined = dot(flipped[c][j], jnp.concatenate(products, axis=1))
        out = [joined[:, k * N : (k + 1) * N] for k in range(len(directions))]
        for d, result in zip(directions, out):
            pieces[2 * c + j, d] = result
        return out

    def outer(c, j):
        return (OUTER_Z[j], OUTER_Y[c], XM, XP)

    def prepare(c, j):
        for k, d in enumerate(outer(c, j)):
            left = dot(flipped[c][j], a_v[c, j, where[c][j][d]])
            lead = left.astype(BF16)
            ahead[2 * c + j, k, :, :N] = lead
            ahead[2 * c + j, k, :, N:] = (left - lead.astype(F32)).astype(BF16)

    def finish(c, j, d):
        block = near(c, j, d)
        result = dot(ahead[2 * c + j, outer(c, j).index(d)], jnp.concatenate([block, block], axis=0))
        pieces[2 * c + j, d] = result
        return result

    def add_up(c, j, directions):
        t = 2 * c + j
        acc = pieces[t, directions[0]] * vector(c, j, directions[0])
        for d in directions[1:]:
            acc += pieces[t, d] * vector(c, j, d)
        return acc

    def apply_here():
        for c in (0, 1):
            for j in (0, 1):
                acc_y[2 * c + j] = add_up(c, j, (SELF, ZM, ZP, INNER_Y[c]))

    def apply_rest(c, j):
        return row_sums(acc_y[2 * c + j] + add_up(c, j, (OUTER_Y[c], XM, XP)))

    for c in (0, 1):
        for j in (0, 1):
            acc_a[2 * c + j] = jnp.abs(form(c, j, SELF, INNER_Z[j], INNER_Y[c])[2])
            prepare(c, j)

    for k in (8, 9, 4, 5):
        sends[k].wait_recv()
    for c in (0, 1):
        for j in (0, 1):
            finish(c, j, OUTER_Z[j])
            acc_a[2 * c + j] += jnp.abs(finish(c, j, OUTER_Y[c]))

    await_arrival(r0.at[4:6], z_recv.at[0])
    below, above = r0[4, 0, 0:4], r0[5, 0, 0:4]
    mine = m0[0, 0:4]
    w_ref[OWN, 0:4] = jnp.where(straddle4 & even4, below, mine)
    w_ref[ZED, 0:4] = jnp.where(even4, below, jnp.where(straddle4, mine, above))
    apply_here()

    for c in (0, 1):
        sends[2 * c].wait_recv()
        sends[2 * c + 1].wait_recv()
        for j in (0, 1):
            acc_a[2 * c + j] += jnp.abs(finish(c, j, XM)) + jnp.abs(finish(c, j, XP))

    sends[6].wait_recv()
    sends[7].wait_recv()
    for c in (0, 1):
        j = 1 - c
        other = pz[1 - c, c]
        mid_self = dot(partner[c, 0], other).astype(BF16)
        mid_outer = dot(partner[c, 1], p_v[c, j]).astype(BF16)
        far = dot(
            jnp.concatenate([other.T, other.T], axis=1),
            jnp.concatenate([mid_self, mid_outer], axis=0),
        )
        t = 2 * c + j
        split = pieces[t, SELF] + pieces[t, OUTER_Z[j]] + far
        whole = (pieces[2 * c, SELF] + pieces[2 * c, ZP]) + (
            pieces[2 * c + 1, SELF] + pieces[2 * c + 1, ZM]
        )
        acc_a[t] += jnp.abs(jnp.where(phase[c] == 1, split, whole))
        for i in (0, 1):
            t = 2 * c + i
            acc_a[t] += jnp.abs(
                jnp.where(phase[c] == 1, pieces[t, INNER_Z[i]], pieces[t, OUTER_Z[i]])
            )

    scales = [row_sums(acc_a[t]) for t in range(4)]

    await_arrival(r0.at[0:4], side_recv.at[0])
    await_arrival(d0, far_recv.at[0])
    for l in range(4):
        moved = (r0[l, 1, 0:4] > 0.5) & even4
        w_ref[2 + l, 0:4] = jnp.where(moved, d0[l, 0, 0:4], r0[l, 0, 0:4])
    sums = [apply_rest(c, j) for c in (0, 1) for j in (0, 1)]

    rhs = rhs_ref[0, :, 0, :]

    def parts(c, lower, upper, extra):
        whole = extra + lower + upper
        split = phase[c] == 1
        return jnp.where(split, lower, whole), jnp.where(split, extra + upper, whole)

    def defects(c, sums):
        return parts(c, -sums[2 * c], -sums[2 * c + 1], rhs[c : c + 1])

    def put(full, swapped, base, pair):
        full[base : base + 1, :] = pair[0]
        full[base + 1 : base + 2, :] = pair[1]
        swapped[base : base + 1, :] = pair[1]
        swapped[base + 1 : base + 2, :] = pair[0]

    def exchange(k, full, swapped, target):
        copies = [
            pltpu.make_async_remote_copy(
                full if r < 4 else swapped, target.at[opposite(r)],
                small_send.at[k], arrival(k, r),
                device_id=devices[r], device_id_type=MESH,
            )
            for r in ORDER
        ]
        for copy in copies:
            copy.start()

    def combined_here(k, full, target, even, straddle):
        await_arrival(target.at[4:6], z_recv.at[k])
        crossing = jnp.where(even, target[4], target[5])
        own = full[...] + jnp.where(straddle, crossing, 0.0)
        return [own, jnp.where(straddle, own, crossing)]

    def combined_rest(k, target, even):
        await_arrival(target.at[0:4], side_recv.at[k])
        await_arrival(target.at[6:14], far_recv.at[k])
        out = []
        for l in range(4):
            far = jnp.where(even, target[6 + 2 * l], target[7 + 2 * l])
            moved = r0[l, 1, 0 : even.shape[0]] > 0.5
            out.append(target[l] + jnp.where(moved, far, 0.0))
        return out

    def first_step(k, total):
        inverse = 1.0 / total[4:8]
        inv_ref[k, 0:4] = inverse
        w_ref[k, 0:4] = w_ref[k, 0:4] + total[0:4] * inverse

    def next_step(k, total):
        w_ref[k, 0:4] = w_ref[k, 0:4] + total * inv_ref[k, 0:4]

    for c in (0, 1):
        put(f1, s1, 2 * c, defects(c, sums))
        put(f1, s1, 4 + 2 * c, parts(c, scales[2 * c], scales[2 * c + 1], EPSILON))
    exchange(1, f1, s1, r1)
    await_arrival(r0, small_send.at[0])
    await_arrival(d0, far_send)
    for copy in sends:
        copy.wait_send()
    for k, total in enumerate(combined_here(1, f1, r1, even8, straddle8)):
        first_step(k, total)
    apply_here()
    for k, total in enumerate(combined_rest(1, r1, even8)):
        first_step(2 + k, total)
    sums = [apply_rest(c, j) for c in (0, 1) for j in (0, 1)]

    for c in (0, 1):
        put(f2, s2, 2 * c, defects(c, sums))
    exchange(2, f2, s2, r2)
    await_arrival(r1, small_send.at[1])
    for k, total in enumerate(combined_here(2, f2, r2, even4, straddle4)):
        next_step(k, total)
    apply_here()
    for k, total in enumerate(combined_rest(2, r2, even4)):
        next_step(2 + k, total)
    lower = [apply_rest(c, 0) for c in (0, 1)]
    for c in (0, 1):
        s3[c : c + 1, :] = -lower[c]
    down = pltpu.make_async_remote_copy(
        s3, r3, small_send.at[3], last_recv, device_id=devices[4], device_id_type=MESH
    )
    down.start()
    await_arrival(r2, small_send.at[2])
    for c in (0, 1):
        out_ref[0, c, 0:1, :] = w_ref[OWN, 2 * c + 1 : 2 * c + 2, :]
    upper = [apply_rest(c, 1) for c in (0, 1)]
    down.wait_recv()
    for c in (0, 1):
        out_ref[0, c, 1:2, :] = (
            rhs[c : c + 1] - upper[c] + jnp.where(phase[c] == 1, r3[c : c + 1, :], -lower[c])
        )

    down.wait_send()


def body(a_blocks, a_cols, p_blocks, agg_ids, coarse_cols, coarse_rhs, coarse_start):
    del coarse_cols
    vmem = pl.BlockSpec(memory_space=pltpu.VMEM)
    hbm = pl.BlockSpec(memory_space=pltpu.HBM)
    one, rows, layers, width = coarse_rhs.shape
    out = pl.pallas_call(
        kernel,
        out_shape=pltpu.VMEM((one, rows, 2 * layers, width), F32),
        in_specs=[hbm] * 6,
        out_specs=vmem,
        scratch_shapes=[
            pltpu.SMEM(a_cols.shape, jnp.int32),
            pltpu.SMEM(agg_ids.shape, jnp.int32),
            pltpu.VMEM(coarse_rhs.shape, F32),
            pltpu.VMEM(coarse_start.shape, F32),
            pltpu.VMEM((2, 2, 7, N, N), BF16),
            pltpu.VMEM((2, 2, N, N), BF16),
            pltpu.VMEM((2, 2, 2, N, N), BF16),
            pltpu.VMEM((2, 2, N, N), BF16),
            pltpu.VMEM((2, 2, N, N), BF16),
            pltpu.VMEM((2, 2, N, N), BF16),
            pltpu.VMEM((2, 2, N, N), BF16),
            pltpu.VMEM((4, 7, N, N), F32),
            pltpu.VMEM((4, N, N), F32),
            pltpu.VMEM((4, N, N), F32),
            pltpu.VMEM((4, 4, N, 2 * N), BF16),
            pltpu.VMEM((6, 8, N), F32),
            pltpu.VMEM((2, 8, N), F32),
            pltpu.VMEM((6, 2, 8, N), F32),
            pltpu.VMEM((4, 2, 8, N), F32),
            pltpu.VMEM((8, N), F32),
            pltpu.VMEM((8, N), F32),
            pltpu.VMEM((14, 8, N), F32),
            pltpu.VMEM((6, 8, N), F32),
            pltpu.VMEM((4, N), F32),
            pltpu.VMEM((4, N), F32),
            pltpu.VMEM((14, 4, N), F32),
            pltpu.VMEM((2, N), F32),
            pltpu.VMEM((2, N), F32),
            pltpu.SemaphoreType.DMA,
            pltpu.SemaphoreType.DMA,
            pltpu.SemaphoreType.DMA((4,)),
            pltpu.SemaphoreType.DMA((10,)),
            pltpu.SemaphoreType.DMA((10,)),
            pltpu.SemaphoreType.DMA((4,)),
            pltpu.SemaphoreType.DMA((3,)),
            pltpu.SemaphoreType.DMA((3,)),
            pltpu.SemaphoreType.DMA,
            pltpu.SemaphoreType.DMA((3,)),
            pltpu.SemaphoreType.DMA,
        ],
        compiler_params=pltpu.CompilerParams(
            collective_id=0, has_side_effects=True, vmem_limit_bytes=63 * 2**20
        ),
        name="coarse_setup",
    )(a_blocks, a_cols, p_blocks, agg_ids, coarse_rhs, coarse_start)
    return out[:, :, 0:1], out[:, :, 1:2]


def solution(mesh):
    return jax.shard_map(
        body,
        mesh=mesh,
        in_specs=(
            P("gx", "gy", "gz", None, None, None),
            P("gx", "gy", "gz", None),
            P("gx", "gy", "gz", None, None),
            P("gx", "gy", "gz"),
            P("gx", "gy", "gz", None),
            P("gx", "gy", "gz", None),
            P("gx", "gy", "gz", None),
        ),
        out_specs=(P("gx", "gy", "gz", None), P("gx", "gy", "gz", None)),
        check_vma=False,
    )
```

```python
import jax
import jax.numpy as jnp
from jax import lax
from jax.experimental import pallas as pl
from jax.experimental.pallas import tpu as pltpu
from jax.sharding import PartitionSpec as P

EPSILON = 1e-05
MESH = pl.DeviceIdType.MESH
F32 = jnp.float32
BF16 = jnp.bfloat16
N = 128
SELF, ZM, ZP, XM, XP, YM, YP = range(7)
OWN, ZED = 0, 1
LATERAL = ((-1, 0), (1, 0), (0, -1), (0, 1))
RELATIONS = (
    [(dx, dy, 0) for dx, dy in LATERAL]
    + [(0, 0, -1), (0, 0, 1)]
    + [(dx, dy, dz) for dx, dy in LATERAL for dz in (-1, 1)]
)


def opposite(r):
    return RELATIONS.index(tuple(-d for d in RELATIONS[r]))


FACES = range(6)
UPWARD = (7, 9, 11, 13)
ORDER = list(range(6, 14)) + [4, 5, 0, 1, 2, 3]


def kernel(
    a_hbm, cols_hbm, p_hbm, agg_hbm, rhs_hbm, start_hbm,
    out_ref,
    cols_ref, agg_ref, rhs_ref, start_ref,
    a_v, p_v, px, py, pz, stage, partner, pieces, acc_a, acc_y, ahead,
    w_ref, m0, r0, d0, f1, s1, r1, inv_ref, f2, s2, r2, s3, r3,
    a_sem, p_sem, in_sem, bulk_send, bulk_recv, small_send, side_recv, z_recv, far_send, far_recv, last_recv,
):
    gx, gy, gz = lax.axis_index("gx"), lax.axis_index("gy"), lax.axis_index("gz")
    nx, ny, nz = lax.axis_size("gx"), lax.axis_size("gy"), lax.axis_size("gz")
    total_y, total_z = 2 * ny, 2 * nz

    def device(r):
        dx, dy, dz = RELATIONS[r]
        return (
            lax.rem(gx + dx + nx, nx) if dx else gx,
            lax.rem(gy + dy + ny, ny) if dy else gy,
            lax.rem(gz + dz + nz, nz) if dz else gz,
        )

    devices = [device(r) for r in range(14)]
    barrier = pltpu.get_barrier_semaphore()
    for r in (6, 8, 10, 12, *FACES):
        pl.semaphore_signal(barrier, inc=1, device_id=devices[r], device_id_type=MESH)

    inputs = [
        pltpu.make_async_copy(source, target, in_sem.at[k])
        for k, (source, target) in enumerate(
            ((agg_hbm, agg_ref), (start_hbm, start_ref), (cols_hbm, cols_ref), (rhs_hbm, rhs_ref))
        )
    ]
    for copy in inputs:
        copy.start()
    p_copy = pltpu.make_async_copy(p_hbm.at[0], p_v, p_sem)
    p_copy.start()
    a_copy = pltpu.make_async_copy(a_hbm.at[0], a_v, a_sem)
    a_copy.start()

    for copy in inputs:
        copy.wait()

    phase = [
        (agg_ref[0, c, 0] != (gx * total_y + 2 * gy + c) * nz + gz).astype(jnp.int32)
        for c in (0, 1)
    ]

    def place(c, j, d):
        dx = {XM: -1, XP: 1}.get(d, 0)
        dy = {YM: -1, YP: 1}.get(d, 0)
        dz = {ZM: -1, ZP: 1}.get(d, 0)
        x = lax.rem(gx + dx + nx, nx)
        y = lax.rem(2 * gy + c + dy + total_y, total_y)
        z = lax.rem(2 * gz + j + dz + total_z, total_z)
        want = (x * total_y + y) * total_z + z
        found = jnp.int32(0)
        for e in range(1, 7):
            found = jnp.where(cols_ref[0, c, j, e] == want, e, found)
        return found

    row8 = lax.broadcasted_iota(jnp.int32, (8, N), 0)
    even8 = lax.rem(row8, 2) == 0
    even4 = even8[0:4]
    ph8 = jnp.where(lax.rem(row8, 4) < 2, phase[0], phase[1]).astype(F32)
    ph4 = ph8[0:4]
    straddle8 = ph8 > 0.5
    straddle4 = ph4 > 0.5
    start = start_ref[0, :, 0, :]
    for c in (0, 1):
        m0[0, 2 * c : 2 * c + 1, :] = start[c : c + 1]
        m0[0, 2 * c + 1 : 2 * c + 2, :] = start[c : c + 1]
    m0[0, 4:8, :] = jnp.zeros((4, N), F32)
    m0[1] = ph8

    where = [[[place(c, j, d) for d in range(7)] for j in (0, 1)] for c in (0, 1)]
    p_copy.wait()
    a_copy.wait()
    stage[0, 0] = a_v[0, 0, where[0][0][SELF]]
    stage[0, 1] = a_v[0, 0, where[0][0][ZM]]
    stage[1, 0] = a_v[1, 1, where[1][1][SELF]]
    stage[1, 1] = a_v[1, 1, where[1][1][ZP]]

    pl.semaphore_wait(barrier, len(FACES) + len(UPWARD))

    def arrival(k, r):
        return (side_recv if r < 4 else z_recv if r < 6 else far_recv).at[k]

    def await_arrival(buffer, semaphore):
        pltpu.make_async_copy(buffer, buffer, semaphore).wait()

    def bulk(k, source, target, r):
        return pltpu.make_async_remote_copy(
            source, target, bulk_send.at[k], bulk_recv.at[k],
            device_id=devices[r], device_id_type=MESH,
        )

    sends = [
        bulk(0, p_v.at[0], px.at[0, 0], 1),
        bulk(1, p_v.at[0], px.at[1, 0], 0),
        bulk(2, p_v.at[1], px.at[0, 1], 1),
        bulk(3, p_v.at[1], px.at[1, 1], 0),
        bulk(4, p_v.at[:, 1], pz.at[0], 5),
        bulk(5, p_v.at[:, 0], pz.at[1], 4),
        bulk(6, stage.at[0], partner.at[0], 4),
        bulk(7, stage.at[1], partner.at[1], 5),
        bulk(8, p_v.at[1], py.at[0], 3),
        bulk(9, p_v.at[0], py.at[1], 2),
    ]
    near_starts = [
        pltpu.make_async_remote_copy(
            m0, r0.at[opposite(r)], small_send.at[0], arrival(0, r),
            device_id=devices[r], device_id_type=MESH,
        )
        for r in FACES
    ]
    far_starts = [
        pltpu.make_async_remote_copy(
            m0, d0.at[opposite(r) // 2 - 3], far_send, far_recv.at[0],
            device_id=devices[r], device_id_type=MESH,
        )
        for r in UPWARD
    ]
    for copy in sends[:4] + far_starts + sends[4:6] + near_starts[4:] + sends[8:] + sends[6:8] + near_starts[:4]:
        copy.start()

    def vector(c, j, d):
        t = 2 * c + j
        if d == SELF:
            block, row = OWN, t
        elif d in (ZM, ZP):
            inner = (d == ZP) == (j == 0)
            block, row = (OWN, 2 * c + 1 - j) if inner else (ZED, t)
        elif d in (XM, XP):
            block, row = 2 + (d - XM), t
        else:
            inner = (d == YP) == (c == 0)
            block, row = (OWN, 2 * (1 - c) + j) if inner else (4 + (d - YM), 2 * (1 - c) + j)
        return w_ref[block, row : row + 1, :]

    def near(c, j, d):
        if d == SELF:
            return p_v[c, j]
        if d in (ZM, ZP):
            inner = (d == ZP) == (j == 0)
            return p_v[c, 1 - j] if inner else pz[0 if d == ZM else 1, c]
        if d in (XM, XP):
            return px[d - XM, c, j]
        inner = (d == YP) == (c == 0)
        return p_v[1 - c, j] if inner else py[d - YM, j]

    def dot(a, b):
        return jnp.dot(a, b, preferred_element_type=F32)

    eye = lax.broadcasted_iota(jnp.int32, (N, N), 0) == lax.broadcasted_iota(
        jnp.int32, (N, N), 1
    )

    def row_sums(block):
        total = jnp.sum(block, axis=1, keepdims=True)
        return jnp.sum(jnp.where(eye, total, 0.0), axis=0, keepdims=True)

    flipped = [[p_v[c, j].T for j in (0, 1)] for c in (0, 1)]

    INNER_Z, OUTER_Z = (ZP, ZM), (ZM, ZP)
    INNER_Y, OUTER_Y = (YP, YM), (YM, YP)

    def form(c, j, *directions):
        products = [
            dot(a_v[c, j, where[c][j][d]], near(c, j, d)).astype(BF16) for d in directions
        ]
        joined = dot(flipped[c][j], jnp.concatenate(products, axis=1))
        out = [joined[:, k * N : (k + 1) * N] for k in range(len(directions))]
        for d, result in zip(directions, out):
            pieces[2 * c + j, d] = result
        return out

    def outer(c, j):
        return (OUTER_Z[j], OUTER_Y[c], XM, XP)

    def prepare(c, j):
        for k, d in enumerate(outer(c, j)):
            left = dot(flipped[c][j], a_v[c, j, where[c][j][d]])
            lead = left.astype(BF16)
            ahead[2 * c + j, k, :, :N] = lead
            ahead[2 * c + j, k, :, N:] = (left - lead.astype(F32)).astype(BF16)

    def finish(c, j, d):
        block = near(c, j, d)
        result = dot(ahead[2 * c + j, outer(c, j).index(d)], jnp.concatenate([block, block], axis=0))
        pieces[2 * c + j, d] = result
        return result

    def add_up(c, j, directions):
        t = 2 * c + j
        acc = pieces[t, directions[0]] * vector(c, j, directions[0])
        for d in directions[1:]:
            acc += pieces[t, d] * vector(c, j, d)
        return acc

    def apply_here():
        for c in (0, 1):
            for j in (0, 1):
                acc_y[2 * c + j] = add_up(c, j, (SELF, ZM, ZP, INNER_Y[c]))

    def apply_rest(c, j):
        return row_sums(acc_y[2 * c + j] + add_up(c, j, (OUTER_Y[c], XM, XP)))

    for c in (0, 1):
        for j in (0, 1):
            acc_a[2 * c + j] = jnp.abs(form(c, j, SELF, INNER_Z[j], INNER_Y[c])[2])
            prepare(c, j)

    for k in (8, 9, 4, 5):
        sends[k].wait_recv()
    for c in (0, 1):
        for j in (0, 1):
            finish(c, j, OUTER_Z[j])
            acc_a[2 * c + j] += jnp.abs(finish(c, j, OUTER_Y[c]))

    await_arrival(r0.at[4:6], z_recv.at[0])
    below, above = r0[4, 0, 0:4], r0[5, 0, 0:4]
    mine = m0[0, 0:4]
    w_ref[OWN, 0:4] = jnp.where(straddle4 & even4, below, mine)
    w_ref[ZED, 0:4] = jnp.where(even4, below, jnp.where(straddle4, mine, above))
    apply_here()

    def finish_x(c):
        for j in (0, 1):
            acc_a[2 * c + j] += jnp.abs(finish(c, j, XM)) + jnp.abs(finish(c, j, XP))

    sends[0].wait_recv()
    sends[1].wait_recv()
    finish_x(0)

    for k in (2, 3, 6, 7):
        sends[k].wait_recv()
    await_arrival(r0.at[0:4], side_recv.at[0])
    await_arrival(d0, far_recv.at[0])
    for l in range(4):
        moved = (r0[l, 1, 0:4] > 0.5) & even4
        w_ref[2 + l, 0:4] = jnp.where(moved, d0[l, 0, 0:4], r0[l, 0, 0:4])
    finish_x(1)
    for c in (0, 1):
        j = 1 - c
        other = pz[1 - c, c]
        mid_self = dot(partner[c, 0], other).astype(BF16)
        mid_outer = dot(partner[c, 1], p_v[c, j]).astype(BF16)
        far = dot(
            jnp.concatenate([other.T, other.T], axis=1),
            jnp.concatenate([mid_self, mid_outer], axis=0),
        )
        t = 2 * c + j
        split = pieces[t, SELF] + pieces[t, OUTER_Z[j]] + far
        whole = (pieces[2 * c, SELF] + pieces[2 * c, ZP]) + (
            pieces[2 * c + 1, SELF] + pieces[2 * c + 1, ZM]
        )
        acc_a[t] += jnp.abs(jnp.where(phase[c] == 1, split, whole))
        for i in (0, 1):
            t = 2 * c + i
            acc_a[t] += jnp.abs(
                jnp.where(phase[c] == 1, pieces[t, INNER_Z[i]], pieces[t, OUTER_Z[i]])
            )

    scales = [row_sums(acc_a[t]) for t in range(4)]

    sums = [apply_rest(c, j) for c in (0, 1) for j in (0, 1)]

    rhs = rhs_ref[0, :, 0, :]

    def parts(c, lower, upper, extra):
        whole = extra + lower + upper
        split = phase[c] == 1
        return jnp.where(split, lower, whole), jnp.where(split, extra + upper, whole)

    def defects(c, sums):
        return parts(c, -sums[2 * c], -sums[2 * c + 1], rhs[c : c + 1])

    def put(full, swapped, base, pair):
        full[base : base + 1, :] = pair[0]
        full[base + 1 : base + 2, :] = pair[1]
        swapped[base : base + 1, :] = pair[1]
        swapped[base + 1 : base + 2, :] = pair[0]

    def exchange(k, full, swapped, target):
        copies = [
            pltpu.make_async_remote_copy(
                full if r < 4 else swapped, target.at[opposite(r)],
                small_send.at[k], arrival(k, r),
                device_id=devices[r], device_id_type=MESH,
            )
            for r in ORDER
        ]
        for copy in copies:
            copy.start()

    def combined_here(k, full, target, even, straddle):
        await_arrival(target.at[4:6], z_recv.at[k])
        crossing = jnp.where(even, target[4], target[5])
        own = full[...] + jnp.where(straddle, crossing, 0.0)
        return [own, jnp.where(straddle, own, crossing)]

    def combined_rest(k, target, even):
        await_arrival(target.at[0:4], side_recv.at[k])
        await_arrival(target.at[6:14], far_recv.at[k])
        out = []
        for l in range(4):
            far = jnp.where(even, target[6 + 2 * l], target[7 + 2 * l])
            moved = r0[l, 1, 0 : even.shape[0]] > 0.5
            out.append(target[l] + jnp.where(moved, far, 0.0))
        return out

    def first_step(k, total):
        inverse = 1.0 / total[4:8]
        inv_ref[k, 0:4] = inverse
        w_ref[k, 0:4] = w_ref[k, 0:4] + total[0:4] * inverse

    def next_step(k, total):
        w_ref[k, 0:4] = w_ref[k, 0:4] + total * inv_ref[k, 0:4]

    for c in (0, 1):
        put(f1, s1, 2 * c, defects(c, sums))
        put(f1, s1, 4 + 2 * c, parts(c, scales[2 * c], scales[2 * c + 1], EPSILON))
    exchange(1, f1, s1, r1)
    await_arrival(r0, small_send.at[0])
    await_arrival(d0, far_send)
    for copy in sends:
        copy.wait_send()
    for k, total in enumerate(combined_here(1, f1, r1, even8, straddle8)):
        first_step(k, total)
    apply_here()
    for k, total in enumerate(combined_rest(1, r1, even8)):
        first_step(2 + k, total)
    sums = [apply_rest(c, j) for c in (0, 1) for j in (0, 1)]

    for c in (0, 1):
        put(f2, s2, 2 * c, defects(c, sums))
    exchange(2, f2, s2, r2)
    await_arrival(r1, small_send.at[1])
    for k, total in enumerate(combined_here(2, f2, r2, even4, straddle4)):
        next_step(k, total)
    apply_here()
    for k, total in enumerate(combined_rest(2, r2, even4)):
        next_step(2 + k, total)
    lower = [apply_rest(c, 0) for c in (0, 1)]
    for c in (0, 1):
        s3[c : c + 1, :] = -lower[c]
    down = pltpu.make_async_remote_copy(
        s3, r3, small_send.at[3], last_recv, device_id=devices[4], device_id_type=MESH
    )
    down.start()
    await_arrival(r2, small_send.at[2])
    for c in (0, 1):
        out_ref[0, c, 0:1, :] = w_ref[OWN, 2 * c + 1 : 2 * c + 2, :]
    upper = [apply_rest(c, 1) for c in (0, 1)]
    down.wait_recv()
    for c in (0, 1):
        out_ref[0, c, 1:2, :] = (
            rhs[c : c + 1] - upper[c] + jnp.where(phase[c] == 1, r3[c : c + 1, :], -lower[c])
        )

    down.wait_send()


def body(a_blocks, a_cols, p_blocks, agg_ids, coarse_cols, coarse_rhs, coarse_start):
    del coarse_cols
    vmem = pl.BlockSpec(memory_space=pltpu.VMEM)
    hbm = pl.BlockSpec(memory_space=pltpu.HBM)
    one, rows, layers, width = coarse_rhs.shape
    out = pl.pallas_call(
        kernel,
        out_shape=pltpu.VMEM((one, rows, 2 * layers, width), F32),
        in_specs=[hbm] * 6,
        out_specs=vmem,
        scratch_shapes=[
            pltpu.SMEM(a_cols.shape, jnp.int32),
            pltpu.SMEM(agg_ids.shape, jnp.int32),
            pltpu.VMEM(coarse_rhs.shape, F32),
            pltpu.VMEM(coarse_start.shape, F32),
            pltpu.VMEM((2, 2, 7, N, N), BF16),
            pltpu.VMEM((2, 2, N, N), BF16),
            pltpu.VMEM((2, 2, 2, N, N), BF16),
            pltpu.VMEM((2, 2, N, N), BF16),
            pltpu.VMEM((2, 2, N, N), BF16),
            pltpu.VMEM((2, 2, N, N), BF16),
            pltpu.VMEM((2, 2, N, N), BF16),
            pltpu.VMEM((4, 7, N, N), F32),
            pltpu.VMEM((4, N, N), F32),
            pltpu.VMEM((4, N, N), F32),
            pltpu.VMEM((4, 4, N, 2 * N), BF16),
            pltpu.VMEM((6, 8, N), F32),
            pltpu.VMEM((2, 8, N), F32),
            pltpu.VMEM((6, 2, 8, N), F32),
            pltpu.VMEM((4, 2, 8, N), F32),
            pltpu.VMEM((8, N), F32),
            pltpu.VMEM((8, N), F32),
            pltpu.VMEM((14, 8, N), F32),
            pltpu.VMEM((6, 8, N), F32),
            pltpu.VMEM((4, N), F32),
            pltpu.VMEM((4, N), F32),
            pltpu.VMEM((14, 4, N), F32),
            pltpu.VMEM((2, N), F32),
            pltpu.VMEM((2, N), F32),
            pltpu.SemaphoreType.DMA,
            pltpu.SemaphoreType.DMA,
            pltpu.SemaphoreType.DMA((4,)),
            pltpu.SemaphoreType.DMA((10,)),
            pltpu.SemaphoreType.DMA((10,)),
            pltpu.SemaphoreType.DMA((4,)),
            pltpu.SemaphoreType.DMA((3,)),
            pltpu.SemaphoreType.DMA((3,)),
            pltpu.SemaphoreType.DMA,
            pltpu.SemaphoreType.DMA((3,)),
            pltpu.SemaphoreType.DMA,
        ],
        compiler_params=pltpu.CompilerParams(
            collective_id=0, has_side_effects=True, vmem_limit_bytes=63 * 2**20
        ),
        name="coarse_setup",
    )(a_blocks, a_cols, p_blocks, agg_ids, coarse_rhs, coarse_start)
    return out[:, :, 0:1], out[:, :, 1:2]


def solution(mesh):
    return jax.shard_map(
        body,
        mesh=mesh,
        in_specs=(
            P("gx", "gy", "gz", None, None, None),
            P("gx", "gy", "gz", None),
            P("gx", "gy", "gz", None, None),
            P("gx", "gy", "gz"),
            P("gx", "gy", "gz", None),
            P("gx", "gy", "gz", None),
            P("gx", "gy", "gz", None),
        ),
        out_specs=(P("gx", "gy", "gz", None), P("gx", "gy", "gz", None)),
        check_vma=False,
    )
```

```python
import jax
import jax.numpy as jnp
from jax import lax
from jax.experimental import pallas as pl
from jax.experimental.pallas import tpu as pltpu
from jax.sharding import PartitionSpec as P

EPSILON = 1e-05
MESH = pl.DeviceIdType.MESH
F32 = jnp.float32
BF16 = jnp.bfloat16
N = 128
SELF, ZM, ZP, XM, XP, YM, YP = range(7)
OWN, ZED = 0, 1
LATERAL = ((-1, 0), (1, 0), (0, -1), (0, 1))
RELATIONS = (
    [(dx, dy, 0) for dx, dy in LATERAL]
    + [(0, 0, -1), (0, 0, 1)]
    + [(dx, dy, dz) for dx, dy in LATERAL for dz in (-1, 1)]
)


def opposite(r):
    return RELATIONS.index(tuple(-d for d in RELATIONS[r]))


FACES = range(6)
UPWARD = (7, 9, 11, 13)
ORDER = list(range(6, 14)) + [4, 5, 0, 1, 2, 3]


def kernel(
    a_hbm, cols_hbm, p_hbm, agg_hbm, rhs_hbm, start_hbm,
    out_ref,
    cols_ref, agg_ref, rhs_ref, start_ref,
    a_v, p_v, px, py, pz, stage, partner, pieces, acc_a, acc_y, ahead,
    w_ref, m0, r0, d0, f1, s1, r1, inv_ref, f2, s2, r2, s3, r3,
    a_sem, p_sem, in_sem, bulk_send, bulk_recv, small_send, side_recv, z_recv, far_send, far_recv, far_y_recv, last_recv,
):
    gx, gy, gz = lax.axis_index("gx"), lax.axis_index("gy"), lax.axis_index("gz")
    nx, ny, nz = lax.axis_size("gx"), lax.axis_size("gy"), lax.axis_size("gz")
    total_y, total_z = 2 * ny, 2 * nz

    def device(r):
        dx, dy, dz = RELATIONS[r]
        return (
            lax.rem(gx + dx + nx, nx) if dx else gx,
            lax.rem(gy + dy + ny, ny) if dy else gy,
            lax.rem(gz + dz + nz, nz) if dz else gz,
        )

    devices = [device(r) for r in range(14)]
    barrier = pltpu.get_barrier_semaphore()
    for r in (6, 8, 10, 12, *FACES):
        pl.semaphore_signal(barrier, inc=1, device_id=devices[r], device_id_type=MESH)

    inputs = [
        pltpu.make_async_copy(source, target, in_sem.at[k])
        for k, (source, target) in enumerate(
            ((agg_hbm, agg_ref), (start_hbm, start_ref), (cols_hbm, cols_ref), (rhs_hbm, rhs_ref))
        )
    ]
    for copy in inputs:
        copy.start()
    p_copy = pltpu.make_async_copy(p_hbm.at[0], p_v, p_sem)
    p_copy.start()
    a_copy = pltpu.make_async_copy(a_hbm.at[0], a_v, a_sem)
    a_copy.start()

    for copy in inputs:
        copy.wait()

    phase = [
        (agg_ref[0, c, 0] != (gx * total_y + 2 * gy + c) * nz + gz).astype(jnp.int32)
        for c in (0, 1)
    ]

    def place(c, j, d):
        dx = {XM: -1, XP: 1}.get(d, 0)
        dy = {YM: -1, YP: 1}.get(d, 0)
        dz = {ZM: -1, ZP: 1}.get(d, 0)
        x = lax.rem(gx + dx + nx, nx)
        y = lax.rem(2 * gy + c + dy + total_y, total_y)
        z = lax.rem(2 * gz + j + dz + total_z, total_z)
        want = (x * total_y + y) * total_z + z
        found = jnp.int32(0)
        for e in range(1, 7):
            found = jnp.where(cols_ref[0, c, j, e] == want, e, found)
        return found

    row8 = lax.broadcasted_iota(jnp.int32, (8, N), 0)
    even8 = lax.rem(row8, 2) == 0
    even4 = even8[0:4]
    ph8 = jnp.where(lax.rem(row8, 4) < 2, phase[0], phase[1]).astype(F32)
    ph4 = ph8[0:4]
    straddle8 = ph8 > 0.5
    straddle4 = ph4 > 0.5
    start = start_ref[0, :, 0, :]
    for c in (0, 1):
        m0[0, 2 * c : 2 * c + 1, :] = start[c : c + 1]
        m0[0, 2 * c + 1 : 2 * c + 2, :] = start[c : c + 1]
    m0[0, 4:8, :] = jnp.zeros((4, N), F32)
    m0[1] = ph8

    where = [[[place(c, j, d) for d in range(7)] for j in (0, 1)] for c in (0, 1)]
    p_copy.wait()
    a_copy.wait()
    stage[0, 0] = a_v[0, 0, where[0][0][SELF]]
    stage[0, 1] = a_v[0, 0, where[0][0][ZM]]
    stage[1, 0] = a_v[1, 1, where[1][1][SELF]]
    stage[1, 1] = a_v[1, 1, where[1][1][ZP]]

    pl.semaphore_wait(barrier, len(FACES) + len(UPWARD))

    def arrival(k, r):
        return (
            side_recv if r < 4 else z_recv if r < 6 else far_recv if r < 10 else far_y_recv
        ).at[k]

    def await_arrival(buffer, semaphore):
        pltpu.make_async_copy(buffer, buffer, semaphore).wait()

    def bulk(k, source, target, r):
        return pltpu.make_async_remote_copy(
            source, target, bulk_send.at[k], bulk_recv.at[k],
            device_id=devices[r], device_id_type=MESH,
        )

    sends = [
        bulk(0, p_v.at[0], px.at[0, 0], 1),
        bulk(1, p_v.at[0], px.at[1, 0], 0),
        bulk(2, p_v.at[1], px.at[0, 1], 1),
        bulk(3, p_v.at[1], px.at[1, 1], 0),
        bulk(4, p_v.at[:, 1], pz.at[0], 5),
        bulk(5, p_v.at[:, 0], pz.at[1], 4),
        bulk(6, stage.at[0], partner.at[0], 4),
        bulk(7, stage.at[1], partner.at[1], 5),
        bulk(8, p_v.at[1], py.at[0], 3),
        bulk(9, p_v.at[0], py.at[1], 2),
    ]
    near_starts = [
        pltpu.make_async_remote_copy(
            m0, r0.at[opposite(r)], small_send.at[0], arrival(0, r),
            device_id=devices[r], device_id_type=MESH,
        )
        for r in FACES
    ]
    far_starts = [
        pltpu.make_async_remote_copy(
            m0, d0.at[opposite(r) // 2 - 3], far_send, far_recv.at[0],
            device_id=devices[r], device_id_type=MESH,
        )
        for r in UPWARD
    ]
    for copy in sends[:4] + far_starts + sends[4:6] + near_starts[4:] + sends[8:] + sends[6:8] + near_starts[:4]:
        copy.start()

    def vector(c, j, d):
        t = 2 * c + j
        if d == SELF:
            block, row = OWN, t
        elif d in (ZM, ZP):
            inner = (d == ZP) == (j == 0)
            block, row = (OWN, 2 * c + 1 - j) if inner else (ZED, t)
        elif d in (XM, XP):
            block, row = 2 + (d - XM), t
        else:
            inner = (d == YP) == (c == 0)
            block, row = (OWN, 2 * (1 - c) + j) if inner else (4 + (d - YM), 2 * (1 - c) + j)
        return w_ref[block, row : row + 1, :]

    def near(c, j, d):
        if d == SELF:
            return p_v[c, j]
        if d in (ZM, ZP):
            inner = (d == ZP) == (j == 0)
            return p_v[c, 1 - j] if inner else pz[0 if d == ZM else 1, c]
        if d in (XM, XP):
            return px[d - XM, c, j]
        inner = (d == YP) == (c == 0)
        return p_v[1 - c, j] if inner else py[d - YM, j]

    def dot(a, b):
        return jnp.dot(a, b, preferred_element_type=F32)

    eye = lax.broadcasted_iota(jnp.int32, (N, N), 0) == lax.broadcasted_iota(
        jnp.int32, (N, N), 1
    )

    def row_sums(block):
        total = jnp.sum(block, axis=1, keepdims=True)
        return jnp.sum(jnp.where(eye, total, 0.0), axis=0, keepdims=True)

    flipped = [[p_v[c, j].T for j in (0, 1)] for c in (0, 1)]

    INNER_Z, OUTER_Z = (ZP, ZM), (ZM, ZP)
    INNER_Y, OUTER_Y = (YP, YM), (YM, YP)

    def form(c, j, *directions):
        products = [
            dot(a_v[c, j, where[c][j][d]], near(c, j, d)).astype(BF16) for d in directions
        ]
        joined = dot(flipped[c][j], jnp.concatenate(products, axis=1))
        out = [joined[:, k * N : (k + 1) * N] for k in range(len(directions))]
        for d, result in zip(directions, out):
            pieces[2 * c + j, d] = result
        return out

    def outer(c, j):
        return (OUTER_Z[j], OUTER_Y[c], XM, XP)

    def prepare(c, j):
        for k, d in enumerate(outer(c, j)):
            left = dot(flipped[c][j], a_v[c, j, where[c][j][d]])
            lead = left.astype(BF16)
            ahead[2 * c + j, k, :, :N] = lead
            ahead[2 * c + j, k, :, N:] = (left - lead.astype(F32)).astype(BF16)

    def finish(c, j, d):
        block = near(c, j, d)
        result = dot(ahead[2 * c + j, outer(c, j).index(d)], jnp.concatenate([block, block], axis=0))
        pieces[2 * c + j, d] = result
        return result

    def add_up(c, j, directions):
        t = 2 * c + j
        acc = pieces[t, directions[0]] * vector(c, j, directions[0])
        for d in directions[1:]:
            acc += pieces[t, d] * vector(c, j, d)
        return acc

    def apply_here():
        for c in (0, 1):
            for j in (0, 1):
                acc_y[2 * c + j] = add_up(c, j, (SELF, ZM, ZP, INNER_Y[c]))

    def apply_y():
        for c in (0, 1):
            for j in (0, 1):
                acc_y[2 * c + j] += add_up(c, j, (OUTER_Y[c],))

    def apply_rest(c, j, *more):
        return row_sums(acc_y[2 * c + j] + add_up(c, j, (*more, XM, XP)))

    for c in (0, 1):
        for j in (0, 1):
            acc_a[2 * c + j] = jnp.abs(form(c, j, SELF, INNER_Z[j], INNER_Y[c])[2])
            prepare(c, j)

    for k in (8, 9, 4, 5):
        sends[k].wait_recv()
    for c in (0, 1):
        for j in (0, 1):
            finish(c, j, OUTER_Z[j])
            acc_a[2 * c + j] += jnp.abs(finish(c, j, OUTER_Y[c]))

    await_arrival(r0.at[4:6], z_recv.at[0])
    below, above = r0[4, 0, 0:4], r0[5, 0, 0:4]
    mine = m0[0, 0:4]
    w_ref[OWN, 0:4] = jnp.where(straddle4 & even4, below, mine)
    w_ref[ZED, 0:4] = jnp.where(even4, below, jnp.where(straddle4, mine, above))
    apply_here()

    def finish_x(c):
        for j in (0, 1):
            acc_a[2 * c + j] += jnp.abs(finish(c, j, XM)) + jnp.abs(finish(c, j, XP))

    sends[0].wait_recv()
    sends[1].wait_recv()
    finish_x(0)

    for k in (2, 3, 6, 7):
        sends[k].wait_recv()
    await_arrival(r0.at[0:4], side_recv.at[0])
    await_arrival(d0, far_recv.at[0])
    for l in range(4):
        moved = (r0[l, 1, 0:4] > 0.5) & even4
        w_ref[2 + l, 0:4] = jnp.where(moved, d0[l, 0, 0:4], r0[l, 0, 0:4])
    finish_x(1)
    for c in (0, 1):
        j = 1 - c
        other = pz[1 - c, c]
        mid_self = dot(partner[c, 0], other).astype(BF16)
        mid_outer = dot(partner[c, 1], p_v[c, j]).astype(BF16)
        far = dot(
            jnp.concatenate([other.T, other.T], axis=1),
            jnp.concatenate([mid_self, mid_outer], axis=0),
        )
        t = 2 * c + j
        split = pieces[t, SELF] + pieces[t, OUTER_Z[j]] + far
        whole = (pieces[2 * c, SELF] + pieces[2 * c, ZP]) + (
            pieces[2 * c + 1, SELF] + pieces[2 * c + 1, ZM]
        )
        acc_a[t] += jnp.abs(jnp.where(phase[c] == 1, split, whole))
        for i in (0, 1):
            t = 2 * c + i
            acc_a[t] += jnp.abs(
                jnp.where(phase[c] == 1, pieces[t, INNER_Z[i]], pieces[t, OUTER_Z[i]])
            )

    scales = [row_sums(acc_a[t]) for t in range(4)]

    sums = [apply_rest(c, j, OUTER_Y[c]) for c in (0, 1) for j in (0, 1)]

    rhs = rhs_ref[0, :, 0, :]

    def parts(c, lower, upper, extra):
        whole = extra + lower + upper
        split = phase[c] == 1
        return jnp.where(split, lower, whole), jnp.where(split, extra + upper, whole)

    def defects(c, sums):
        return parts(c, -sums[2 * c], -sums[2 * c + 1], rhs[c : c + 1])

    def put(full, swapped, base, pair):
        full[base : base + 1, :] = pair[0]
        full[base + 1 : base + 2, :] = pair[1]
        swapped[base : base + 1, :] = pair[1]
        swapped[base + 1 : base + 2, :] = pair[0]

    def exchange(k, full, swapped, target):
        copies = [
            pltpu.make_async_remote_copy(
                full if r < 4 else swapped, target.at[opposite(r)],
                small_send.at[k], arrival(k, r),
                device_id=devices[r], device_id_type=MESH,
            )
            for r in ORDER
        ]
        for copy in copies:
            copy.start()

    def combined_here(k, full, target, even, straddle):
        await_arrival(target.at[4:6], z_recv.at[k])
        crossing = jnp.where(even, target[4], target[5])
        own = full[...] + jnp.where(straddle, crossing, 0.0)
        return [own, jnp.where(straddle, own, crossing)]

    def combined_sides(k, target, even, low):
        await_arrival(
            target.at[6 + 2 * low : 10 + 2 * low], (far_y_recv if low else far_recv).at[k]
        )
        out = []
        for l in (low, low + 1):
            far = jnp.where(even, target[6 + 2 * l], target[7 + 2 * l])
            moved = r0[l, 1, 0 : even.shape[0]] > 0.5
            out.append((2 + l, target[l] + jnp.where(moved, far, 0.0)))
        return out

    def first_step(k, total):
        inverse = 1.0 / total[4:8]
        inv_ref[k, 0:4] = inverse
        w_ref[k, 0:4] = w_ref[k, 0:4] + total[0:4] * inverse

    def next_step(k, total):
        w_ref[k, 0:4] = w_ref[k, 0:4] + total * inv_ref[k, 0:4]

    for c in (0, 1):
        put(f1, s1, 2 * c, defects(c, sums))
        put(f1, s1, 4 + 2 * c, parts(c, scales[2 * c], scales[2 * c + 1], EPSILON))
    exchange(1, f1, s1, r1)
    await_arrival(r0, small_send.at[0])
    await_arrival(d0, far_send)
    for copy in sends:
        copy.wait_send()
    for k, total in enumerate(combined_here(1, f1, r1, even8, straddle8)):
        first_step(k, total)
    apply_here()
    await_arrival(r1.at[0:4], side_recv.at[1])
    for k, total in combined_sides(1, r1, even8, 2):
        first_step(k, total)
    apply_y()
    for k, total in combined_sides(1, r1, even8, 0):
        first_step(k, total)
    sums = [apply_rest(c, j) for c in (0, 1) for j in (0, 1)]

    for c in (0, 1):
        put(f2, s2, 2 * c, defects(c, sums))
    exchange(2, f2, s2, r2)
    await_arrival(r1, small_send.at[1])
    for k, total in enumerate(combined_here(2, f2, r2, even4, straddle4)):
        next_step(k, total)
    apply_here()
    await_arrival(r2.at[0:4], side_recv.at[2])
    for k, total in combined_sides(2, r2, even4, 2):
        next_step(k, total)
    apply_y()
    for k, total in combined_sides(2, r2, even4, 0):
        next_step(k, total)
    lower = [apply_rest(c, 0) for c in (0, 1)]
    for c in (0, 1):
        s3[c : c + 1, :] = -lower[c]
    down = pltpu.make_async_remote_copy(
        s3, r3, small_send.at[3], last_recv, device_id=devices[4], device_id_type=MESH
    )
    down.start()
    await_arrival(r2, small_send.at[2])
    for c in (0, 1):
        out_ref[0, c, 0:1, :] = w_ref[OWN, 2 * c + 1 : 2 * c + 2, :]
    upper = [apply_rest(c, 1) for c in (0, 1)]
    down.wait_recv()
    for c in (0, 1):
        out_ref[0, c, 1:2, :] = (
            rhs[c : c + 1] - upper[c] + jnp.where(phase[c] == 1, r3[c : c + 1, :], -lower[c])
        )

    down.wait_send()


def body(a_blocks, a_cols, p_blocks, agg_ids, coarse_cols, coarse_rhs, coarse_start):
    del coarse_cols
    vmem = pl.BlockSpec(memory_space=pltpu.VMEM)
    hbm = pl.BlockSpec(memory_space=pltpu.HBM)
    one, rows, layers, width = coarse_rhs.shape
    out = pl.pallas_call(
        kernel,
        out_shape=pltpu.VMEM((one, rows, 2 * layers, width), F32),
        in_specs=[hbm] * 6,
        out_specs=vmem,
        scratch_shapes=[
            pltpu.SMEM(a_cols.shape, jnp.int32),
            pltpu.SMEM(agg_ids.shape, jnp.int32),
            pltpu.VMEM(coarse_rhs.shape, F32),
            pltpu.VMEM(coarse_start.shape, F32),
            pltpu.VMEM((2, 2, 7, N, N), BF16),
            pltpu.VMEM((2, 2, N, N), BF16),
            pltpu.VMEM((2, 2, 2, N, N), BF16),
            pltpu.VMEM((2, 2, N, N), BF16),
            pltpu.VMEM((2, 2, N, N), BF16),
            pltpu.VMEM((2, 2, N, N), BF16),
            pltpu.VMEM((2, 2, N, N), BF16),
            pltpu.VMEM((4, 7, N, N), F32),
            pltpu.VMEM((4, N, N), F32),
            pltpu.VMEM((4, N, N), F32),
            pltpu.VMEM((4, 4, N, 2 * N), BF16),
            pltpu.VMEM((6, 8, N), F32),
            pltpu.VMEM((2, 8, N), F32),
            pltpu.VMEM((6, 2, 8, N), F32),
            pltpu.VMEM((4, 2, 8, N), F32),
            pltpu.VMEM((8, N), F32),
            pltpu.VMEM((8, N), F32),
            pltpu.VMEM((14, 8, N), F32),
            pltpu.VMEM((6, 8, N), F32),
            pltpu.VMEM((4, N), F32),
            pltpu.VMEM((4, N), F32),
            pltpu.VMEM((14, 4, N), F32),
            pltpu.VMEM((2, N), F32),
            pltpu.VMEM((2, N), F32),
            pltpu.SemaphoreType.DMA,
            pltpu.SemaphoreType.DMA,
            pltpu.SemaphoreType.DMA((4,)),
            pltpu.SemaphoreType.DMA((10,)),
            pltpu.SemaphoreType.DMA((10,)),
            pltpu.SemaphoreType.DMA((4,)),
            pltpu.SemaphoreType.DMA((3,)),
            pltpu.SemaphoreType.DMA((3,)),
            pltpu.SemaphoreType.DMA,
            pltpu.SemaphoreType.DMA((3,)),
            pltpu.SemaphoreType.DMA((3,)),
            pltpu.SemaphoreType.DMA,
        ],
        compiler_params=pltpu.CompilerParams(
            collective_id=0, has_side_effects=True, vmem_limit_bytes=63 * 2**20
        ),
        name="coarse_setup",
    )(a_blocks, a_cols, p_blocks, agg_ids, coarse_rhs, coarse_start)
    return out[:, :, 0:1], out[:, :, 1:2]


def solution(mesh):
    return jax.shard_map(
        body,
        mesh=mesh,
        in_specs=(
            P("gx", "gy", "gz", None, None, None),
            P("gx", "gy", "gz", None),
            P("gx", "gy", "gz", None, None),
            P("gx", "gy", "gz"),
            P("gx", "gy", "gz", None),
            P("gx", "gy", "gz", None),
            P("gx", "gy", "gz", None),
        ),
        out_specs=(P("gx", "gy", "gz", None), P("gx", "gy", "gz", None)),
        check_vma=False,
    )
```

```python
import jax
import jax.numpy as jnp
from jax import lax
from jax.experimental import pallas as pl
from jax.experimental.pallas import tpu as pltpu
from jax.sharding import PartitionSpec as P

EPSILON = 1e-05
MESH = pl.DeviceIdType.MESH
F32 = jnp.float32
BF16 = jnp.bfloat16
N = 128
SELF, ZM, ZP, XM, XP, YM, YP = range(7)
OWN, ZED = 0, 1
LATERAL = ((-1, 0), (1, 0), (0, -1), (0, 1))
RELATIONS = (
    [(dx, dy, 0) for dx, dy in LATERAL]
    + [(0, 0, -1), (0, 0, 1)]
    + [(dx, dy, dz) for dx, dy in LATERAL for dz in (-1, 1)]
)


def opposite(r):
    return RELATIONS.index(tuple(-d for d in RELATIONS[r]))


FACES = range(6)
UPWARD = (7, 9, 11, 13)
ORDER = list(range(6, 14)) + [4, 5, 0, 1, 2, 3]


def kernel(
    a_hbm, cols_hbm, p_hbm, agg_hbm, rhs_hbm, start_hbm,
    out_ref,
    cols_ref, agg_ref, rhs_ref, start_ref,
    a_v, p_v, px, py, pz, stage, partner, pieces, acc_a, acc_y, ahead,
    w_ref, m0, r0, d0, f1, s1, r1, inv_ref, f2, s2, r2, s3, r3,
    a_sem, p_sem, in_sem, bulk_send, bulk_recv, small_send, side_recv, z_recv, far_send, far_recv, far_y_recv, last_recv,
):
    gx, gy, gz = lax.axis_index("gx"), lax.axis_index("gy"), lax.axis_index("gz")
    nx, ny, nz = lax.axis_size("gx"), lax.axis_size("gy"), lax.axis_size("gz")
    total_y, total_z = 2 * ny, 2 * nz

    def device(r):
        dx, dy, dz = RELATIONS[r]
        return (
            lax.rem(gx + dx + nx, nx) if dx else gx,
            lax.rem(gy + dy + ny, ny) if dy else gy,
            lax.rem(gz + dz + nz, nz) if dz else gz,
        )

    devices = [device(r) for r in range(14)]
    barrier = pltpu.get_barrier_semaphore()
    for r in (6, 8, 10, 12, *FACES):
        pl.semaphore_signal(barrier, inc=1, device_id=devices[r], device_id_type=MESH)

    inputs = [
        pltpu.make_async_copy(source, target, in_sem.at[k])
        for k, (source, target) in enumerate(
            ((agg_hbm, agg_ref), (start_hbm, start_ref), (cols_hbm, cols_ref), (rhs_hbm, rhs_ref))
        )
    ]
    for copy in inputs:
        copy.start()
    p_copy = pltpu.make_async_copy(p_hbm.at[0], p_v, p_sem)
    p_copy.start()
    a_copy = pltpu.make_async_copy(a_hbm.at[0], a_v, a_sem)
    a_copy.start()

    for copy in inputs:
        copy.wait()

    phase = [
        (agg_ref[0, c, 0] != (gx * total_y + 2 * gy + c) * nz + gz).astype(jnp.int32)
        for c in (0, 1)
    ]

    def place(c, j, d):
        dx = {XM: -1, XP: 1}.get(d, 0)
        dy = {YM: -1, YP: 1}.get(d, 0)
        dz = {ZM: -1, ZP: 1}.get(d, 0)
        x = lax.rem(gx + dx + nx, nx)
        y = lax.rem(2 * gy + c + dy + total_y, total_y)
        z = lax.rem(2 * gz + j + dz + total_z, total_z)
        want = (x * total_y + y) * total_z + z
        found = jnp.int32(0)
        for e in range(1, 7):
            found = jnp.where(cols_ref[0, c, j, e] == want, e, found)
        return found

    row8 = lax.broadcasted_iota(jnp.int32, (8, N), 0)
    even8 = lax.rem(row8, 2) == 0
    even4 = even8[0:4]
    ph8 = jnp.where(lax.rem(row8, 4) < 2, phase[0], phase[1]).astype(F32)
    ph4 = ph8[0:4]
    straddle8 = ph8 > 0.5
    straddle4 = ph4 > 0.5
    start = start_ref[0, :, 0, :]
    for c in (0, 1):
        m0[0, 2 * c : 2 * c + 1, :] = start[c : c + 1]
        m0[0, 2 * c + 1 : 2 * c + 2, :] = start[c : c + 1]
    m0[0, 4:8, :] = jnp.zeros((4, N), F32)
    m0[1] = ph8

    where = [[[place(c, j, d) for d in range(7)] for j in (0, 1)] for c in (0, 1)]
    p_copy.wait()
    a_copy.wait()
    stage[0, 0] = a_v[0, 0, where[0][0][SELF]]
    stage[0, 1] = a_v[0, 0, where[0][0][ZM]]
    stage[1, 0] = a_v[1, 1, where[1][1][SELF]]
    stage[1, 1] = a_v[1, 1, where[1][1][ZP]]

    pl.semaphore_wait(barrier, len(FACES) + len(UPWARD))

    def arrival(k, r):
        return (
            side_recv if r < 4 else z_recv if r < 6 else far_recv if r < 10 else far_y_recv
        ).at[k]

    def await_arrival(buffer, semaphore):
        pltpu.make_async_copy(buffer, buffer, semaphore).wait()

    def bulk(k, source, target, r):
        return pltpu.make_async_remote_copy(
            source, target, bulk_send.at[k], bulk_recv.at[k],
            device_id=devices[r], device_id_type=MESH,
        )

    sends = [
        bulk(0, p_v.at[0], px.at[0, 0], 1),
        bulk(1, p_v.at[0], px.at[1, 0], 0),
        bulk(2, p_v.at[1], px.at[0, 1], 1),
        bulk(3, p_v.at[1], px.at[1, 1], 0),
        bulk(4, p_v.at[:, 1], pz.at[0], 5),
        bulk(5, p_v.at[:, 0], pz.at[1], 4),
        bulk(6, stage.at[0], partner.at[0], 4),
        bulk(7, stage.at[1], partner.at[1], 5),
        bulk(8, p_v.at[1], py.at[0], 3),
        bulk(9, p_v.at[0], py.at[1], 2),
    ]
    near_starts = [
        pltpu.make_async_remote_copy(
            m0, r0.at[opposite(r)], small_send.at[0], arrival(0, r),
            device_id=devices[r], device_id_type=MESH,
        )
        for r in FACES
    ]
    far_starts = [
        pltpu.make_async_remote_copy(
            m0, d0.at[opposite(r) // 2 - 3], far_send, far_recv.at[0],
            device_id=devices[r], device_id_type=MESH,
        )
        for r in UPWARD
    ]
    for copy in sends[:4] + far_starts + sends[4:6] + near_starts[4:] + sends[8:] + sends[6:8] + near_starts[:4]:
        copy.start()

    def vector(c, j, d):
        t = 2 * c + j
        if d == SELF:
            block, row = OWN, t
        elif d in (ZM, ZP):
            inner = (d == ZP) == (j == 0)
            block, row = (OWN, 2 * c + 1 - j) if inner else (ZED, t)
        elif d in (XM, XP):
            block, row = 2 + (d - XM), t
        else:
            inner = (d == YP) == (c == 0)
            block, row = (OWN, 2 * (1 - c) + j) if inner else (4 + (d - YM), 2 * (1 - c) + j)
        return w_ref[block, row : row + 1, :]

    def near(c, j, d):
        if d == SELF:
            return p_v[c, j]
        if d in (ZM, ZP):
            inner = (d == ZP) == (j == 0)
            return p_v[c, 1 - j] if inner else pz[0 if d == ZM else 1, c]
        if d in (XM, XP):
            return px[d - XM, c, j]
        inner = (d == YP) == (c == 0)
        return p_v[1 - c, j] if inner else py[d - YM, j]

    def dot(a, b):
        return jnp.dot(a, b, preferred_element_type=F32)

    eye = lax.broadcasted_iota(jnp.int32, (N, N), 0) == lax.broadcasted_iota(
        jnp.int32, (N, N), 1
    )

    def row_sums(block):
        total = jnp.sum(block, axis=1, keepdims=True)
        return jnp.sum(jnp.where(eye, total, 0.0), axis=0, keepdims=True)

    flipped = [[p_v[c, j].T for j in (0, 1)] for c in (0, 1)]

    INNER_Z, OUTER_Z = (ZP, ZM), (ZM, ZP)
    INNER_Y, OUTER_Y = (YP, YM), (YM, YP)

    def form(c, j, *directions):
        products = [
            dot(a_v[c, j, where[c][j][d]], near(c, j, d)).astype(BF16) for d in directions
        ]
        joined = dot(flipped[c][j], jnp.concatenate(products, axis=1))
        out = [joined[:, k * N : (k + 1) * N] for k in range(len(directions))]
        for d, result in zip(directions, out):
            pieces[2 * c + j, d] = result
        return out

    def outer(c, j):
        return (OUTER_Z[j], OUTER_Y[c], XM, XP)

    def prepare(c, j):
        for k, d in enumerate(outer(c, j)):
            left = dot(flipped[c][j], a_v[c, j, where[c][j][d]])
            lead = left.astype(BF16)
            ahead[2 * c + j, k, :, :N] = lead
            ahead[2 * c + j, k, :, N:] = (left - lead.astype(F32)).astype(BF16)

    def finish(c, j, d):
        block = near(c, j, d)
        result = dot(ahead[2 * c + j, outer(c, j).index(d)], jnp.concatenate([block, block], axis=0))
        pieces[2 * c + j, d] = result
        return result

    def add_up(c, j, directions):
        t = 2 * c + j
        acc = pieces[t, directions[0]] * vector(c, j, directions[0])
        for d in directions[1:]:
            acc += pieces[t, d] * vector(c, j, d)
        return acc

    def apply_here():
        for c in (0, 1):
            for j in (0, 1):
                acc_y[2 * c + j] = add_up(c, j, (SELF, ZM, ZP, INNER_Y[c]))

    def apply_y():
        for c in (0, 1):
            for j in (0, 1):
                acc_y[2 * c + j] += add_up(c, j, (OUTER_Y[c],))

    def apply_rest(c, j, *more):
        return row_sums(acc_y[2 * c + j] + add_up(c, j, (*more, XM, XP)))

    for c in (0, 1):
        for j in (0, 1):
            acc_a[2 * c + j] = jnp.abs(form(c, j, SELF, INNER_Z[j], INNER_Y[c])[2])
            prepare(c, j)

    for k in (8, 9, 4, 5):
        sends[k].wait_recv()
    for c in (0, 1):
        for j in (0, 1):
            finish(c, j, OUTER_Z[j])
            acc_a[2 * c + j] += jnp.abs(finish(c, j, OUTER_Y[c]))

    await_arrival(r0.at[4:6], z_recv.at[0])
    below, above = r0[4, 0, 0:4], r0[5, 0, 0:4]
    mine = m0[0, 0:4]
    w_ref[OWN, 0:4] = jnp.where(straddle4 & even4, below, mine)
    w_ref[ZED, 0:4] = jnp.where(even4, below, jnp.where(straddle4, mine, above))
    apply_here()

    for c in (0, 1):
        for i in (0, 1):
            t = 2 * c + i
            acc_a[t] += jnp.abs(
                jnp.where(phase[c] == 1, pieces[t, INNER_Z[i]], pieces[t, OUTER_Z[i]])
            )

    def finish_x(c):
        for j in (0, 1):
            acc_a[2 * c + j] += jnp.abs(finish(c, j, XM)) + jnp.abs(finish(c, j, XP))

    sends[0].wait_recv()
    sends[1].wait_recv()
    finish_x(0)
    first_scale = row_sums(acc_a[0])

    for k in (2, 3, 6, 7):
        sends[k].wait_recv()
    await_arrival(r0.at[0:4], side_recv.at[0])
    await_arrival(d0, far_recv.at[0])
    for l in range(4):
        moved = (r0[l, 1, 0:4] > 0.5) & even4
        w_ref[2 + l, 0:4] = jnp.where(moved, d0[l, 0, 0:4], r0[l, 0, 0:4])
    finish_x(1)
    for c in (0, 1):
        j = 1 - c
        other = pz[1 - c, c]
        mid_self = dot(partner[c, 0], other).astype(BF16)
        mid_outer = dot(partner[c, 1], p_v[c, j]).astype(BF16)
        far = dot(
            jnp.concatenate([other.T, other.T], axis=1),
            jnp.concatenate([mid_self, mid_outer], axis=0),
        )
        t = 2 * c + j
        split = pieces[t, SELF] + pieces[t, OUTER_Z[j]] + far
        whole = (pieces[2 * c, SELF] + pieces[2 * c, ZP]) + (
            pieces[2 * c + 1, SELF] + pieces[2 * c + 1, ZM]
        )
        acc_a[t] += jnp.abs(jnp.where(phase[c] == 1, split, whole))

    scales = [first_scale] + [row_sums(acc_a[t]) for t in (1, 2, 3)]

    sums = [apply_rest(c, j, OUTER_Y[c]) for c in (0, 1) for j in (0, 1)]

    rhs = rhs_ref[0, :, 0, :]

    def parts(c, lower, upper, extra):
        whole = extra + lower + upper
        split = phase[c] == 1
        return jnp.where(split, lower, whole), jnp.where(split, extra + upper, whole)

    def defects(c, sums):
        return parts(c, -sums[2 * c], -sums[2 * c + 1], rhs[c : c + 1])

    def put(full, swapped, base, pair):
        full[base : base + 1, :] = pair[0]
        full[base + 1 : base + 2, :] = pair[1]
        swapped[base : base + 1, :] = pair[1]
        swapped[base + 1 : base + 2, :] = pair[0]

    def exchange(k, full, swapped, target):
        copies = [
            pltpu.make_async_remote_copy(
                full if r < 4 else swapped, target.at[opposite(r)],
                small_send.at[k], arrival(k, r),
                device_id=devices[r], device_id_type=MESH,
            )
            for r in ORDER
        ]
        for copy in copies:
            copy.start()

    def combined_here(k, full, target, even, straddle):
        await_arrival(target.at[4:6], z_recv.at[k])
        crossing = jnp.where(even, target[4], target[5])
        own = full[...] + jnp.where(straddle, crossing, 0.0)
        return [own, jnp.where(straddle, own, crossing)]

    def combined_sides(k, target, even, low):
        await_arrival(
            target.at[6 + 2 * low : 10 + 2 * low], (far_y_recv if low else far_recv).at[k]
        )
        out = []
        for l in (low, low + 1):
            far = jnp.where(even, target[6 + 2 * l], target[7 + 2 * l])
            moved = r0[l, 1, 0 : even.shape[0]] > 0.5
            out.append((2 + l, target[l] + jnp.where(moved, far, 0.0)))
        return out

    def first_step(k, total):
        inverse = 1.0 / total[4:8]
        inv_ref[k, 0:4] = inverse
        w_ref[k, 0:4] = w_ref[k, 0:4] + total[0:4] * inverse

    def next_step(k, total):
        w_ref[k, 0:4] = w_ref[k, 0:4] + total * inv_ref[k, 0:4]

    for c in (0, 1):
        put(f1, s1, 2 * c, defects(c, sums))
        put(f1, s1, 4 + 2 * c, parts(c, scales[2 * c], scales[2 * c + 1], EPSILON))
    exchange(1, f1, s1, r1)
    await_arrival(r0, small_send.at[0])
    await_arrival(d0, far_send)
    for copy in sends:
        copy.wait_send()
    for k, total in enumerate(combined_here(1, f1, r1, even8, straddle8)):
        first_step(k, total)
    apply_here()
    await_arrival(r1.at[0:4], side_recv.at[1])
    for k, total in combined_sides(1, r1, even8, 2):
        first_step(k, total)
    apply_y()
    for k, total in combined_sides(1, r1, even8, 0):
        first_step(k, total)
    sums = [apply_rest(c, j) for c in (0, 1) for j in (0, 1)]

    for c in (0, 1):
        put(f2, s2, 2 * c, defects(c, sums))
    exchange(2, f2, s2, r2)
    await_arrival(r1, small_send.at[1])
    for k, total in enumerate(combined_here(2, f2, r2, even4, straddle4)):
        next_step(k, total)
    apply_here()
    await_arrival(r2.at[0:4], side_recv.at[2])
    for k, total in combined_sides(2, r2, even4, 2):
        next_step(k, total)
    apply_y()
    for k, total in combined_sides(2, r2, even4, 0):
        next_step(k, total)
    lower = [apply_rest(c, 0) for c in (0, 1)]
    for c in (0, 1):
        s3[c : c + 1, :] = -lower[c]
    down = pltpu.make_async_remote_copy(
        s3, r3, small_send.at[3], last_recv, device_id=devices[4], device_id_type=MESH
    )
    down.start()
    await_arrival(r2, small_send.at[2])
    for c in (0, 1):
        out_ref[0, c, 0:1, :] = w_ref[OWN, 2 * c + 1 : 2 * c + 2, :]
    upper = [apply_rest(c, 1) for c in (0, 1)]
    down.wait_recv()
    for c in (0, 1):
        out_ref[0, c, 1:2, :] = (
            rhs[c : c + 1] - upper[c] + jnp.where(phase[c] == 1, r3[c : c + 1, :], -lower[c])
        )

    down.wait_send()


def body(a_blocks, a_cols, p_blocks, agg_ids, coarse_cols, coarse_rhs, coarse_start):
    del coarse_cols
    vmem = pl.BlockSpec(memory_space=pltpu.VMEM)
    hbm = pl.BlockSpec(memory_space=pltpu.HBM)
    one, rows, layers, width = coarse_rhs.shape
    out = pl.pallas_call(
        kernel,
        out_shape=pltpu.VMEM((one, rows, 2 * layers, width), F32),
        in_specs=[hbm] * 6,
        out_specs=vmem,
        scratch_shapes=[
            pltpu.SMEM(a_cols.shape, jnp.int32),
            pltpu.SMEM(agg_ids.shape, jnp.int32),
            pltpu.VMEM(coarse_rhs.shape, F32),
            pltpu.VMEM(coarse_start.shape, F32),
            pltpu.VMEM((2, 2, 7, N, N), BF16),
            pltpu.VMEM((2, 2, N, N), BF16),
            pltpu.VMEM((2, 2, 2, N, N), BF16),
            pltpu.VMEM((2, 2, N, N), BF16),
            pltpu.VMEM((2, 2, N, N), BF16),
            pltpu.VMEM((2, 2, N, N), BF16),
            pltpu.VMEM((2, 2, N, N), BF16),
            pltpu.VMEM((4, 7, N, N), F32),
            pltpu.VMEM((4, N, N), F32),
            pltpu.VMEM((4, N, N), F32),
            pltpu.VMEM((4, 4, N, 2 * N), BF16),
            pltpu.VMEM((6, 8, N), F32),
            pltpu.VMEM((2, 8, N), F32),
            pltpu.VMEM((6, 2, 8, N), F32),
            pltpu.VMEM((4, 2, 8, N), F32),
            pltpu.VMEM((8, N), F32),
            pltpu.VMEM((8, N), F32),
            pltpu.VMEM((14, 8, N), F32),
            pltpu.VMEM((6, 8, N), F32),
            pltpu.VMEM((4, N), F32),
            pltpu.VMEM((4, N), F32),
            pltpu.VMEM((14, 4, N), F32),
            pltpu.VMEM((2, N), F32),
            pltpu.VMEM((2, N), F32),
            pltpu.SemaphoreType.DMA,
            pltpu.SemaphoreType.DMA,
            pltpu.SemaphoreType.DMA((4,)),
            pltpu.SemaphoreType.DMA((10,)),
            pltpu.SemaphoreType.DMA((10,)),
            pltpu.SemaphoreType.DMA((4,)),
            pltpu.SemaphoreType.DMA((3,)),
            pltpu.SemaphoreType.DMA((3,)),
            pltpu.SemaphoreType.DMA,
            pltpu.SemaphoreType.DMA((3,)),
            pltpu.SemaphoreType.DMA((3,)),
            pltpu.SemaphoreType.DMA,
        ],
        compiler_params=pltpu.CompilerParams(
            collective_id=0, has_side_effects=True, vmem_limit_bytes=63 * 2**20
        ),
        name="coarse_setup",
    )(a_blocks, a_cols, p_blocks, agg_ids, coarse_rhs, coarse_start)
    return out[:, :, 0:1], out[:, :, 1:2]


def solution(mesh):
    return jax.shard_map(
        body,
        mesh=mesh,
        in_specs=(
            P("gx", "gy", "gz", None, None, None),
            P("gx", "gy", "gz", None),
            P("gx", "gy", "gz", None, None),
            P("gx", "gy", "gz"),
            P("gx", "gy", "gz", None),
            P("gx", "gy", "gz", None),
            P("gx", "gy", "gz", None),
        ),
        out_specs=(P("gx", "gy", "gz", None), P("gx", "gy", "gz", None)),
        check_vma=False,
    )
```
